256 devices in a mesh: seq: 32 (over z_hi, x, core), chan: 8 (over z_lo, y).
Axes of the slice: x: 4, y: 4, z: 8 (z_hi: 4, z_lo: 2; z = z_hi * 2 + z_lo), core: 2. Of those that a mesh axis runs over, the one named last changes fastest.
Arguments:
- inputs: bfloat16 [4096, 4096], P(('seq', 'chan')), may hold values from -6 to 6
- grad_output: bfloat16 [4096, 4096], P(('seq', 'chan')), may hold values from -0.09375 to 0.09375
- filter_taps: float32 [384, 4096], P('seq', 'chan'), may hold values from -18.973665 to 18.973665
Outputs:
- grad_inputs: bfloat16 [4096, 4096], P(('seq', 'chan'))
- grad_filter: float32 [384, 4096], P('seq', 'chan')
The draws below stay inside these ranges and needn't reach their ends.
All inputs are finite; a program needn't handle non-finite values.
Results may differ from the reference program's by a relative error of at most 0.001.
Values may be sent and summed in bfloat16 or wider, within the bound.
A program may use at most 64 MiB of HBM per device.

```python
import math
import jax
import jax.numpy as jnp
from jax import lax

CH = 4096
TOKENS = 4096
FL = 384


def block_levels(stream_key, dims, split, low, top_value):
    factor_of = 1.0
    for dim, parts in split:
        steps = jax.random.uniform(jax.random.fold_in(jax.random.fold_in(stream_key, 6), dim), (parts,), jnp.float32, low / len(split), top_value / len(split))
        factor_of = factor_of * jnp.repeat(jnp.exp(steps), dims[dim] // parts).reshape((-1,) + (1,) * (len(dims) - 1 - dim))
    return factor_of


def noise(own_key, extent, spread, bound, cuts=(), dtype=jnp.bfloat16):
    values = spread * jax.random.normal(own_key, extent, jnp.float32)
    if cuts:
        values = values * block_levels(own_key, extent, cuts, -0.22, 0.18)
    return jnp.clip(values, -bound, bound).astype(dtype)


def setup_inputs(seed: int = 0) -> dict:
    arg_keys = jax.random.split(jax.random.key(seed), 4)
    return {
        "inputs": noise(arg_keys[0], (TOKENS, CH), 1.0, 6.0, ((0, 256),)),
        "grad_output": noise(arg_keys[1], (TOKENS, CH), (TOKENS ** -0.5), 0.09375, ((0, 256),)),
        "filter_taps": noise(arg_keys[2], (FL, CH), ((TOKENS // FL) ** 0.5), 18.973665, ((0, 32), (1, 8)), jnp.float32),
    }


def reference(inputs, grad_output, filter_taps):
    seq_len = inputs.shape[0]
    lag_total = filter_taps.shape[0]
    channels = inputs.shape[1]
    fft_len = 1
    while fft_len < seq_len + lag_total:
        fft_len = fft_len * 2
    group = math.gcd(channels, 256)
    batches = channels // group

    def regroup(array):
        return jnp.transpose(array.astype(jnp.float32).reshape(array.shape[0], batches, group), (1, 0, 2))

    def correlate(pieces):
        in_blk, grad_blk, tap_blk = pieces
        in_spec = jnp.fft.rfft(in_blk, n=fft_len, axis=0)
        grad_spec = jnp.fft.rfft(grad_blk, n=fft_len, axis=0)
        tap_spec = jnp.fft.rfft(tap_blk, n=fft_len, axis=0)
        grad_in = jnp.fft.irfft(jnp.conj(tap_spec) * grad_spec, n=fft_len, axis=0)[:seq_len]
        grad_tap = jnp.fft.irfft(grad_spec * jnp.conj(in_spec), n=fft_len, axis=0)[:lag_total]
        return grad_in.astype(jnp.float32), grad_tap.astype(jnp.float32)

    grad_in, grad_tap = lax.map(correlate, (regroup(inputs), regroup(grad_output), regroup(filter_taps)))
    grad_inputs = jnp.transpose(grad_in, (1, 0, 2)).reshape(seq_len, channels).astype(jnp.bfloat16)
    grad_filter = jnp.transpose(grad_tap, (1, 0, 2)).reshape(lag_total, channels).astype(jnp.float32)
    return grad_inputs, grad_filter
```

```python
import functools

import jax
import jax.numpy as jnp
from jax import lax
from jax.experimental import pallas as pl
from jax.experimental.pallas import tpu as pltpu
from jax.sharding import PartitionSpec as P

MESH = pl.DeviceIdType.MESH
F32 = jnp.float32
BF16 = jnp.bfloat16
LANES = 128
CORES = 2

G_ONE, X_ONE, TAPS, G_TWO, X_TWO, GI_TWO, GI_ONE, GF = range(8)


def contract(lhs, rhs, lhs_dim, rhs_dim):
    return lax.dot_general(
        lhs, rhs, (((lhs_dim,), (rhs_dim,)), ((), ())), preferred_element_type=F32
    )


def swap_chunks(tile):
    row = lax.broadcasted_iota(jnp.int32, tile.shape, 0)
    chunk = lax.broadcasted_iota(jnp.int32, tile.shape, 1) // 16
    for bit in (1, 2, 4):
        row_set = (row & bit) != 0
        chunk_set = (chunk & bit) != 0
        below = pltpu.roll(pltpu.roll(tile, 8 - bit, 0), 16 * bit, 1)
        above = pltpu.roll(pltpu.roll(tile, bit, 0), LANES - 16 * bit, 1)
        moved = jnp.where(chunk_set, below, above)
        tile = jnp.where(row_set == chunk_set, tile, moved)
    return tile


def kernel(
    x_hbm, g_hbm, taps_ref, gi_out, gf_out,
    g_one, x_one, g_send, x_send, g_two, x_two,
    tap_send, tap_recv, tap_rows, tap_tiles, toeplitz,
    g_wide, x_wide, g_cat, gi_wide, gi_send, gi_two, gi_turn,
    gf_tiles, gf_rows, gf_send, gf_recv,
    send_sem, recv_sem,
):
    seqs = lax.axis_size("seq")
    chans = lax.axis_size("chan")
    seq = lax.axis_index("seq")
    chan = lax.axis_index("chan")
    core = lax.rem(seq, CORES)
    block = lax.div(seq, CORES)
    blocks = seqs // CORES
    near = core * chans + chan
    nears = CORES * chans
    column = core * blocks + block
    width = g_one.shape[2]

    barrier = pltpu.get_barrier_semaphore()

    def greet_seq(step, carry):
        pl.semaphore_signal(
            barrier, inc=1, device_id={"seq": lax.rem(seq + step, seqs), "chan": chan}, device_id_type=MESH
        )
        return carry

    def greet_near(step, carry):
        other = lax.rem(chan + step, chans)
        for other_core in range(CORES):
            pl.semaphore_signal(
                barrier, inc=1, device_id={"seq": block * CORES + other_core, "chan": other}, device_id_type=MESH
            )
        return carry

    lax.fori_loop(1, chans, greet_near, 0)
    lax.fori_loop(1, seqs, greet_seq, 0)

    lags = taps_ref.shape[0]
    for tile in range(taps_ref.shape[1] // LANES):
        lanes = slice(tile * LANES, (tile + 1) * LANES)
        first = swap_chunks(taps_ref[0:8, lanes])
        last = jnp.concatenate([taps_ref[8:lags, lanes], jnp.zeros((16 - lags, LANES), F32)], axis=0)
        last = swap_chunks(last)
        tap_send[8 * tile : 8 * tile + 8, 0, :] = first
        tap_send[8 * tile : 8 * tile + 8, 1, :] = last

    row = lax.broadcasted_iota(jnp.int32, (width, width), 0)
    lane = lax.broadcasted_iota(jnp.int32, (width, width), 1)
    eye = (row == lane).astype(F32).astype(BF16)
    flip = ((row ^ lane) == LANES - 1).astype(F32).astype(BF16)

    pl.semaphore_wait(barrier, seqs - 1 + CORES * (chans - 1))

    def remote(src, dst, which, to_seq, to_chan):
        pltpu.make_async_remote_copy(
            src_ref=src, dst_ref=dst, send_sem=send_sem.at[which], recv_sem=recv_sem.at[which],
            device_id={"seq": to_seq, "chan": to_chan}, device_id_type=MESH,
        ).start()

    def local(src, dst, which):
        pltpu.make_async_copy(src, dst, recv_sem.at[which]).start()

    def received(ref, which):
        pltpu.make_async_copy(ref, ref, recv_sem.at[which]).wait()

    def sent(ref, which):
        part = ref.at[pl.ds(0, ref.shape[0] - 1)]
        pltpu.make_async_copy(part, part, send_sem.at[which]).wait()

    def columns_of(ref, index):
        other_core = lax.div(index, chans)
        other_chan = lax.rem(index, chans)
        start = pl.multiple_of(other_chan * (CORES * width) + other_core * width, width)
        return ref.at[:, pl.ds(start, width)]

    def to_near(src_of, dst, which):
        def step(shift, carry):
            index = lax.rem(near + shift, nears)
            remote(src_of(index), dst, which, block * CORES + lax.div(index, chans), lax.rem(index, chans))
            return carry

        lax.fori_loop(1, nears, step, 0)
        local(src_of(near), dst, which)

    def to_far(src, dst, which):
        def step(shift, carry):
            index = lax.rem(block + shift, blocks)
            remote(src.at[index], dst.at[block], which, index * CORES + core, chan)
            return carry

        lax.fori_loop(1, blocks, step, 0)
        local(src.at[block], dst.at[block], which)

    to_near(functools.partial(columns_of, g_hbm), g_one.at[near], G_ONE)

    def send_taps(step, carry):
        index = lax.rem(seq + step, seqs)
        slot = lax.rem(index, CORES) * blocks + lax.div(index, CORES)
        remote(tap_send.at[slot], tap_recv.at[seq], TAPS, index, chan)
        return carry

    lax.fori_loop(1, seqs, send_taps, 0)
    local(tap_send.at[column], tap_recv.at[seq], TAPS)
    to_near(functools.partial(columns_of, x_hbm), x_one.at[near], X_ONE)

    received(g_one, G_ONE)
    turned = contract(eye, g_one[...].reshape(width, width), 1, 1)
    g_send[...] = turned.astype(BF16).reshape(g_send.shape)
    to_far(g_send, g_two, G_TWO)

    received(x_one, X_ONE)
    turned = contract(eye, x_one[...].reshape(width, width), 1, 1).astype(BF16)
    turned = contract(turned, flip, 1, 0)
    x_send[...] = turned.astype(BF16).reshape(x_send.shape)
    to_far(x_send, x_two, X_TWO)

    received(tap_recv, TAPS)
    for part in range(2):
        rows = tap_recv[:, part, :]
        for lag in range(8 if part == 0 else lags - 8):
            shifted = rows if lag == 0 else pltpu.roll(rows, LANES - 16 * lag, 1)
            tap_rows[pl.ds(8 * part + lag, seqs, stride=lags), :] = shifted
    tap_count = tap_rows.shape[0] // LANES
    group = tap_tiles.shape[1]
    for tile in range(tap_count):
        tap_tiles[tile] = tap_rows[tile * LANES : (tile + 1) * LANES, :].T[0:group, :]

    row = lax.broadcasted_iota(jnp.int32, (LANES, LANES), 0)
    lane = lax.broadcasted_iota(jnp.int32, (LANES, LANES), 1)
    above = lane >= row
    nothing = jnp.zeros((LANES, LANES), F32)

    def build(channel, carry):
        rolled = []
        for tile in range(tap_count):
            values = jnp.broadcast_to(tap_tiles[tile, pl.ds(channel, 1), :], (LANES, LANES))
            rolled.append(pltpu.roll(values, 0, 1, stride=1, stride_axis=0))
        for tile in range(tap_count + 1):
            upper = rolled[tile] if tile < tap_count else nothing
            lower = rolled[tile - 1] if tile > 0 else nothing
            values = jnp.where(above, upper, lower)
            high = values.astype(BF16)
            low = (values - high.astype(F32)).astype(BF16)
            toeplitz[channel, 0:LANES, tile * LANES : (tile + 1) * LANES] = high
            toeplitz[channel, LANES : 2 * LANES, tile * LANES : (tile + 1) * LANES] = low
        return carry

    lax.fori_loop(0, group, build, 0)

    all_rows = blocks * group
    received(g_two, G_TWO)
    values = g_two[...].reshape(all_rows, width).astype(F32)
    for half in range(2):
        g_wide[half, 0:all_rows, :] = values[:, half * LANES : (half + 1) * LANES]
        g_wide[half, all_rows : all_rows + 2 * group, :] = jnp.zeros((2 * group, LANES), F32)

    def strided(channel, ahead=0):
        return pl.ds(channel + ahead * group, blocks, stride=group)

    def inputs_step(channel, carry):
        even = [g_wide[0, strided(channel, ahead), :].astype(BF16) for ahead in range(3)]
        odd = [g_wide[1, strided(channel, ahead), :].astype(BF16) for ahead in range(2)]
        top = jnp.concatenate([even[0], odd[0], even[1], odd[1]], axis=1)
        bottom = jnp.concatenate([odd[0], even[1], odd[1], even[2]], axis=1)
        both = jnp.concatenate([top, bottom], axis=0)
        g_cat[channel] = both
        result = contract(both, toeplitz[channel], 1, 1)
        result = result[:, 0:LANES] + result[:, LANES : 2 * LANES]
        gi_wide[0, strided(channel), :] = result[0:blocks]
        gi_wide[1, strided(channel), :] = result[blocks : 2 * blocks]
        return carry

    lax.fori_loop(0, group, inputs_step, 0)
    for half in range(2):
        gi_send[:, :, half * LANES : (half + 1) * LANES] = (
            gi_wide[half].astype(BF16).reshape(blocks, group, LANES)
        )
    to_far(gi_send, gi_two, GI_TWO)

    received(x_two, X_TWO)
    values = x_two[...].reshape(all_rows, width).astype(F32)
    for half in range(2):
        x_wide[half] = values[:, half * LANES : (half + 1) * LANES]
    keep = lane <= row

    def filter_step(channel, carry):
        both = jnp.concatenate(
            [x_wide[0, strided(channel), :], x_wide[1, strided(channel), :]], axis=0
        ).astype(BF16)
        product = contract(both, g_cat[channel], 0, 0)
        rolled = [
            pltpu.roll(product[:, tile * LANES : (tile + 1) * LANES], 1, 1, stride=1, stride_axis=0)
            for tile in range(tap_count + 1)
        ]
        for tile in range(tap_count):
            total = jnp.where(keep, rolled[tile], rolled[tile + 1])
            gf_tiles[tile, pl.ds(channel, 1), :] = jnp.sum(total, axis=0, keepdims=True)
        return carry

    lax.fori_loop(0, group, filter_step, 0)
    for tile in range(tap_count):
        gf_rows[tile * LANES : (tile + 1) * LANES, :] = gf_tiles[tile].T
    first_chunk = lax.broadcasted_iota(jnp.int32, (seqs, LANES), 1) < group
    for part in range(2):
        packed = jnp.zeros((seqs, LANES), F32)
        for lag in range(8 if part == 0 else lags - 8):
            rows = jnp.where(first_chunk, gf_rows[pl.ds(8 * part + lag, seqs, stride=lags), :], 0.0)
            packed = packed + (rows if lag == 0 else pltpu.roll(rows, 16 * lag, 1))
        gf_send[:, part, :] = packed

    def send_filter(step, carry):
        index = lax.rem(seq + step, seqs)
        remote(gf_send.at[index], gf_recv.at[column], GF, index, chan)
        return carry

    lax.fori_loop(1, seqs, send_filter, 0)
    local(gf_send.at[seq], gf_recv.at[column], GF)

    received(gi_two, GI_TWO)
    turned = contract(eye, gi_two[...].reshape(width, width), 1, 1)
    gi_turn[...] = turned.astype(BF16).reshape(gi_turn.shape)
    to_near(lambda index: gi_turn.at[index], columns_of(gi_out, near), GI_ONE)

    received(gf_recv, GF)
    for part in range(2):
        rows = gf_recv[:, part, :]
        count = 8 if part == 0 else lags - 8
        for tile in range(seqs // 8):
            values = swap_chunks(rows[8 * tile : 8 * tile + 8])
            gf_out[8 * part : 8 * part + count, tile * LANES : (tile + 1) * LANES] = values[0:count]

    received(gi_out, GI_ONE)
    for ref, which in (
        (g_one, G_ONE), (x_one, X_ONE), (tap_send, TAPS), (g_send, G_TWO), (x_send, X_TWO),
        (gi_send, GI_TWO), (gi_turn, GI_ONE), (gf_send, GF),
    ):
        sent(ref, which)


def per_device(inputs, grad_output, filter_taps, seqs, chans):
    rows, channels = inputs.shape
    lags = filter_taps.shape[0]
    nears = CORES * chans
    blocks = seqs // CORES
    width = channels // nears
    group = width // blocks
    total_lags = lags * seqs
    tiles = total_lags // LANES
    exchange = pltpu.VMEM((16, 16, width), BF16)
    return pl.pallas_call(
        kernel,
        out_shape=(
            jax.ShapeDtypeStruct(inputs.shape, BF16),
            jax.ShapeDtypeStruct(filter_taps.shape, F32),
        ),
        in_specs=[
            pl.BlockSpec(memory_space=pl.ANY),
            pl.BlockSpec(memory_space=pl.ANY),
            pl.BlockSpec(memory_space=pltpu.VMEM),
        ],
        out_specs=(
            pl.BlockSpec(memory_space=pl.ANY),
            pl.BlockSpec(memory_space=pltpu.VMEM),
        ),
        scratch_shapes=[
            exchange, exchange, exchange, exchange, exchange, exchange,
            pltpu.VMEM((seqs, 2, LANES), F32),
            pltpu.VMEM((seqs, 2, LANES), F32),
            pltpu.VMEM((total_lags, LANES), F32),
            pltpu.VMEM((tiles, group, LANES), F32),
            pltpu.VMEM((group, 2 * LANES, total_lags + LANES), BF16),
            pltpu.VMEM((2, (blocks + 2) * group, LANES), F32),
            pltpu.VMEM((2, blocks * group, LANES), F32),
            pltpu.VMEM((group, 2 * blocks, total_lags + LANES), BF16),
            pltpu.VMEM((2, blocks * group, LANES), F32),
            exchange, exchange, exchange,
            pltpu.VMEM((tiles, LANES, LANES), F32),
            pltpu.VMEM((total_lags, LANES), F32),
            pltpu.VMEM((seqs, 2, LANES), F32),
            pltpu.VMEM((seqs, 2, LANES), F32),
            pltpu.SemaphoreType.DMA((8,)),
            pltpu.SemaphoreType.DMA((8,)),
        ],
        compiler_params=pltpu.CompilerParams(
            collective_id=0, has_side_effects=True, vmem_limit_bytes=40 * 1024 * 1024
        ),
    )(inputs, grad_output, filter_taps)


def solution(mesh):
    return jax.shard_map(
        functools.partial(per_device, seqs=mesh.shape["seq"], chans=mesh.shape["chan"]),
        mesh=mesh,
        in_specs=(P(("seq", "chan"), None), P(("seq", "chan"), None), P("seq", "chan")),
        out_specs=(P(("seq", "chan"), None), P("seq", "chan")),
        check_vma=False,
    )
```

```python
import functools

import jax
import jax.numpy as jnp
from jax import lax
from jax.experimental import pallas as pl
from jax.experimental.pallas import tpu as pltpu
from jax.sharding import PartitionSpec as P

MESH = pl.DeviceIdType.MESH
F32 = jnp.float32
BF16 = jnp.bfloat16
LANES = 128
HALF = LANES // 2
CORES = 2
ROW = 4
PLANES = 4
SHORT = 32
FOLDS = LANES // SHORT
UNROLL = 4

G_ONE, X_ONE, TAPS, G_TWO, X_TWO, HALO_FIRST, HALO_LAST, GI_TWO, GI_ONE, GF, TAPS_IN, GF_OUT = range(12)


def contract(lhs, rhs, lhs_dim, rhs_dim):
    return lax.dot_general(
        lhs, rhs, (((lhs_dim,), (rhs_dim,)), ((), ())), preferred_element_type=F32
    )


def left(values, by):
    return values if by % LANES == 0 else pltpu.roll(values, LANES - by % LANES, 1)


def kernel(
    x_hbm, g_hbm, taps_hbm, gi_out, gf_out,
    g_one, x_one, g_send, x_send, g_two, x_two,
    taps, tap_send, tap_recv, tap_rows, tap_tiles, toeplitz,
    g_wide, x_wide, g_cat, gi_wide, gi_send, gi_two, gi_turn,
    gf_partial, gf_rows, gf_send, gf_recv, gf_own,
    send_sem, recv_sem,
):
    seqs = lax.axis_size("seq")
    chans = lax.axis_size("chan")
    seq = lax.axis_index("seq")
    chan = lax.axis_index("chan")
    core = lax.rem(seq, CORES)
    block = lax.div(seq, CORES)
    plane = lax.div(block, ROW)
    place = lax.rem(block, ROW)
    near = core * chans + chan
    nears = CORES * chans
    columns = CORES * ROW
    column = core * ROW + place
    width = g_one.shape[2]
    lags = taps_hbm.shape[0]
    half_lags = lags // 2
    tap_count = tap_tiles.shape[0]
    group = tap_tiles.shape[1]
    rows_of_x = 2 * ROW

    def received(ref, which):
        pltpu.make_async_copy(ref, ref, recv_sem.at[which]).wait()

    def sent(ref, which):
        pltpu.make_async_copy(ref, ref, send_sem.at[which]).wait()

    def remote(src, dst, which, to_seq, to_chan):
        pltpu.make_async_remote_copy(
            src_ref=src, dst_ref=dst, send_sem=send_sem.at[which], recv_sem=recv_sem.at[which],
            device_id={"seq": to_seq, "chan": to_chan}, device_id_type=MESH,
        ).start()

    def local(src, dst, which):
        pltpu.make_async_copy(src, dst, recv_sem.at[which]).start()

    with jax.named_scope("greet"):
        local(taps_hbm, taps, TAPS_IN)
        barrier = pltpu.get_barrier_semaphore()

        def greet_seq(step, carry):
            pl.semaphore_signal(
                barrier, inc=1, device_id={"seq": lax.rem(seq + step, seqs), "chan": chan}, device_id_type=MESH
            )
            return carry

        def greet_near(step, carry):
            other = lax.rem(chan + step, chans)
            for other_core in range(CORES):
                pl.semaphore_signal(
                    barrier, inc=1, device_id={"seq": block * CORES + other_core, "chan": other}, device_id_type=MESH
                )
            return carry

        lax.fori_loop(1, seqs, greet_seq, 0)
        lax.fori_loop(1, chans, greet_near, 0)

    first_half = lax.broadcasted_iota(jnp.int32, (8, LANES), 1) < HALF

    with jax.named_scope("pack_taps"):
        received(taps, TAPS_IN)
        nothing = jnp.zeros((8 - half_lags, LANES), F32)
        for tile in range(columns // 2):
            lanes = slice(tile * LANES, (tile + 1) * LANES)
            early = jnp.concatenate([taps[0:half_lags, lanes], nothing], axis=0)
            late = jnp.concatenate([taps[half_lags:lags, lanes], nothing], axis=0)
            tap_send[2 * tile] = jnp.where(first_half, early, left(late, HALF))
            tap_send[2 * tile + 1] = jnp.where(first_half, left(early, HALF), late)

    row = lax.broadcasted_iota(jnp.int32, (width, width), 0)
    lane = lax.broadcasted_iota(jnp.int32, (width, width), 1)
    eye = (row == lane).astype(F32).astype(BF16)
    flip = ((row ^ lane) == LANES - 1).astype(F32).astype(BF16)

    with jax.named_scope("barrier"):
        pl.semaphore_wait(barrier, seqs - 1 + CORES * (chans - 1))

    def columns_of(ref, index):
        other_core = lax.div(index, chans)
        other_chan = lax.rem(index, chans)
        start = pl.multiple_of(other_chan * (CORES * width) + other_core * width, width)
        return ref.at[:, pl.ds(start, width)]

    def to_near(src_of, dst, which):
        def step(shift, carry):
            index = lax.rem(near + shift, nears)
            remote(src_of(index), dst, which, block * CORES + lax.div(index, chans), lax.rem(index, chans))
            return carry

        lax.fori_loop(1, nears, step, 0)
        local(src_of(near), dst, which)

    def to_row(src, dst, which):
        for shift in range(1, ROW):
            index = lax.rem(place + shift, ROW)
            remote(src.at[index], dst.at[place], which, (plane * ROW + index) * CORES + core, chan)
        local(src.at[place], dst.at[place], which)

    def to_seq(src_of, dst, which):
        def step(shift, carry):
            index = lax.rem(seq + shift, seqs)
            remote(src_of(index), dst, which, index, chan)
            return carry

        lax.fori_loop(1, seqs, step, 0)
        local(src_of(seq), dst, which)

    def column_of(index):
        return lax.rem(index, CORES) * ROW + lax.rem(lax.div(index, CORES), ROW)

    with jax.named_scope("send_one"):
        to_near(functools.partial(columns_of, g_hbm), g_one.at[near], G_ONE)
        to_seq(lambda index: tap_send.at[column_of(index)], tap_recv.at[seq], TAPS)
        to_near(functools.partial(columns_of, x_hbm), x_one.at[near], X_ONE)

    with jax.named_scope("turn_g"):
        received(g_one, G_ONE)
        turned = contract(eye, g_one[...].reshape(width, width), 1, 1)
        g_send[...] = turned.astype(BF16).reshape(g_send.shape)

    with jax.named_scope("send_g_two"):
        to_row(g_send, g_two, G_TWO)

        def send_halo(src, dst, which):
            for index in range(ROW):
                remote(src.at[index], dst, which, ((plane - 1) * ROW + index) * CORES + core, chan)

        @pl.when((plane > 0) & (place == 0))
        def _():
            send_halo(g_send, g_two.at[ROW], HALO_FIRST)

        @pl.when((plane > 0) & (place == 1))
        def _():
            send_halo(g_send.at[:, :, 0:LANES], g_two.at[ROW + 1, :, 0:LANES], HALO_LAST)

    with jax.named_scope("turn_x"):
        received(x_one, X_ONE)
        turned = contract(eye, x_one[...].reshape(width, width), 1, 1).astype(BF16)
        turned = contract(turned, flip, 1, 0)
        x_send[...] = turned.astype(BF16).reshape(x_send.shape)
        to_row(x_send, x_two, X_TWO)

    with jax.named_scope("unpack_taps"):
        received(tap_recv, TAPS)
        for lag in range(half_lags):
            rows = tap_recv[:, lag, :]
            tap_rows[pl.ds(lag, seqs, stride=lags), :] = rows
            tap_rows[pl.ds(half_lags + lag, seqs, stride=lags), :] = left(rows, HALF)
        for tile in range(tap_count):
            tap_tiles[tile] = tap_rows[tile * LANES : (tile + 1) * LANES, :].T[0:group, :]

    row = lax.broadcasted_iota(jnp.int32, (SHORT, LANES), 0)
    lane = lax.broadcasted_iota(jnp.int32, (SHORT, LANES), 1)
    ahead = lane >= row
    nothing = jnp.zeros((SHORT, LANES), F32)

    def build(channel):
        rolled = []
        for tile in range(tap_count):
            values = jnp.broadcast_to(tap_tiles[tile, pl.ds(channel, 1), :], (SHORT, LANES))
            rolled.append(pltpu.roll(values, 0, 1, stride=1, stride_axis=0))
        for tile in range(tap_count + 1):
            upper = rolled[tile] if tile < tap_count else nothing
            lower = rolled[tile - 1] if tile > 0 else nothing
            values = jnp.where(ahead, upper, lower)
            high = values.astype(BF16)
            low = (values - high.astype(F32)).astype(BF16)
            toeplitz[channel, 0:SHORT, tile * LANES : (tile + 1) * LANES] = high
            toeplitz[channel, SHORT : 2 * SHORT, tile * LANES : (tile + 1) * LANES] = low

    def for_channels(body):
        def step(first, carry):
            for extra in range(UNROLL):
                body(first * UNROLL + extra)
            return carry

        lax.fori_loop(0, group // UNROLL, step, 0)

    with jax.named_scope("toeplitz"):
        for_channels(build)

    def widen(source, target, slots):
        for slot in slots:
            for half in range(2):
                start = (2 * slot + half) * group
                target[start : start + group, :] = source[slot, :, half * LANES : (half + 1) * LANES].astype(F32)

    with jax.named_scope("widen_g"):
        received(g_two.at[pl.ds(0, ROW)], G_TWO)
        widen(g_two, g_wide, range(ROW))

        @pl.when(plane < PLANES - 1)
        def _():
            received(g_two.at[ROW], HALO_FIRST)
            received(g_two.at[ROW + 1, :, 0:LANES], HALO_LAST)
            widen(g_two, g_wide, (ROW,))
            g_wide[(rows_of_x + 2) * group : (rows_of_x + 3) * group, :] = g_two[ROW + 1, :, 0:LANES].astype(F32)

        @pl.when(plane == PLANES - 1)
        def _():
            g_wide[rows_of_x * group : (rows_of_x + 3) * group, :] = jnp.zeros((3 * group, LANES), F32)

    with jax.named_scope("widen_x"):
        received(x_two, X_TWO)
        widen(x_two, x_wide, range(ROW))

    def strided(channel, blocks_ahead=0):
        return pl.ds(channel + blocks_ahead * group, rows_of_x, stride=group)

    lane_of_row = lax.broadcasted_iota(jnp.int32, (rows_of_x, LANES), 1)
    keep = lane - row < LANES - SHORT + 1

    def filter_step(channel):
        blocks = [g_wide[strided(channel, tile), :] for tile in range(tap_count + 1)]
        folds = []
        for fold in range(FOLDS):
            shifted = [left(values, SHORT * fold) for values in blocks]
            if fold > 0:
                near_end = lane_of_row < LANES - SHORT * fold
                shifted = [
                    jnp.where(near_end, shifted[tile], shifted[tile + 1]) for tile in range(tap_count)
                ] + [shifted[tap_count]]
            folds.append(jnp.concatenate(shifted, axis=1))
        windows = jnp.concatenate(folds, axis=0).astype(BF16)
        g_cat[channel] = windows
        source = x_wide[strided(channel), :]
        mine = jnp.concatenate(
            [left(source, LANES - SHORT * (fold + 1)) for fold in range(FOLDS)], axis=0
        ).astype(BF16)
        product = contract(mine[:, 0:SHORT], windows, 0, 0)
        rolled = [
            pltpu.roll(
                product[:, tile * LANES : (tile + 1) * LANES], LANES - SHORT + 1, 1, stride=1, stride_axis=0
            )
            for tile in range(tap_count + 1)
        ]
        for tile in range(tap_count):
            total = jnp.where(keep, rolled[tile], rolled[tile + 1])
            total = (total[0:8] + total[8:16]) + (total[16:24] + total[24:32])
            gf_partial[tile, pl.ds(pl.multiple_of(channel * 8, 8), 8), :] = total

    with jax.named_scope("grad_filter"):
        for_channels(filter_step)

    with jax.named_scope("send_gf"):
        for tile in range(tap_count):
            total = gf_partial[tile, pl.ds(0, group, stride=8), :]
            for part in range(1, 8):
                total = total + gf_partial[tile, pl.ds(part, group, stride=8), :]
            total = jnp.concatenate([total, jnp.zeros((LANES - group, LANES), F32)], axis=0)
            gf_rows[tile * LANES : (tile + 1) * LANES, :] = total.T
        for lag in range(half_lags):
            early = gf_rows[pl.ds(lag, seqs, stride=lags), :]
            late = gf_rows[pl.ds(half_lags + lag, seqs, stride=lags), :]
            gf_send[:, lag, :] = early + left(late, HALF)
        for lag in range(half_lags, 8):
            gf_send[:, lag, :] = jnp.zeros((seqs, LANES), F32)
        to_seq(lambda index: gf_send.at[index], gf_recv.at[plane * columns + column], GF)

    def inputs_step(channel):
        result = contract(g_cat[channel], toeplitz[channel], 1, 1)
        result = jnp.concatenate([result, jnp.zeros((SHORT, LANES - 2 * SHORT), F32)], axis=1)
        result = result + left(result, SHORT)
        total = result[0:rows_of_x]
        for fold in range(1, FOLDS):
            part = pltpu.roll(result[fold * rows_of_x : (fold + 1) * rows_of_x], SHORT * fold, 1)
            total = jnp.where(lane_of_row < SHORT * fold, total, part)
        gi_wide[strided(channel), :] = total

    with jax.named_scope("grad_inputs"):
        for_channels(inputs_step)

    with jax.named_scope("send_gi_two"):
        for slot in range(ROW):
            for half in range(2):
                start = (2 * slot + half) * group
                gi_send[slot, :, half * LANES : (half + 1) * LANES] = gi_wide[start : start + group, :].astype(BF16)
        to_row(gi_send, gi_two, GI_TWO)

    with jax.named_scope("turn_gi"):
        received(gi_two, GI_TWO)
        turned = contract(eye, gi_two[...].reshape(width, width), 1, 1)
        gi_turn[...] = turned.astype(BF16).reshape(gi_turn.shape)
        to_near(lambda index: gi_turn.at[index], columns_of(gi_out, near), GI_ONE)

    with jax.named_scope("unpack_gf"):
        received(gf_recv, GF)
        sums = []
        for index in range(columns):
            total = gf_recv[index]
            for other in range(1, PLANES):
                total = total + gf_recv[other * columns + index]
            sums.append(total)
        for tile in range(columns // 2):
            lanes = slice(tile * LANES, (tile + 1) * LANES)
            early = jnp.where(first_half, sums[2 * tile], left(sums[2 * tile + 1], HALF))
            late = jnp.where(first_half, left(sums[2 * tile], HALF), sums[2 * tile + 1])
            gf_own[0:half_lags, lanes] = early[0:half_lags]
            gf_own[half_lags:lags, lanes] = late[0:half_lags]
        local(gf_own, gf_out, GF_OUT)

    with jax.named_scope("finish"):
        for ref, which in (
            (g_one, G_ONE), (x_one, X_ONE), (tap_recv, TAPS), (g_send, G_TWO), (x_send, X_TWO),
            (gi_send, GI_TWO), (gi_turn, GI_ONE), (gf_send, GF),
        ):
            sent(ref.at[pl.ds(0, ref.shape[0] - 1)], which)

        @pl.when((plane > 0) & (place == 0))
        def _():
            sent(g_send, HALO_FIRST)

        @pl.when((plane > 0) & (place == 1))
        def _():
            sent(g_send.at[:, :, 0:LANES], HALO_LAST)

        received(gf_out, GF_OUT)
        received(gi_out, GI_ONE)


def per_device(inputs, grad_output, filter_taps, seqs, chans):
    rows, channels = inputs.shape
    lags, tap_channels = filter_taps.shape
    nears = CORES * chans
    width = channels // nears
    group = width // ROW
    columns = CORES * ROW
    total_lags = lags * seqs
    tiles = total_lags // LANES
    window = total_lags + LANES
    one = pltpu.VMEM((nears, rows, width), BF16)
    two = pltpu.VMEM((ROW, group, width), BF16)
    return pl.pallas_call(
        kernel,
        out_shape=(
            jax.ShapeDtypeStruct(inputs.shape, BF16),
            jax.ShapeDtypeStruct(filter_taps.shape, F32),
        ),
        in_specs=[pl.BlockSpec(memory_space=pl.ANY)] * 3,
        out_specs=(pl.BlockSpec(memory_space=pl.ANY), pl.BlockSpec(memory_space=pl.ANY)),
        scratch_shapes=[
            one, one, two, two,
            pltpu.VMEM((ROW + 2, group, width), BF16),
            two,
            pltpu.VMEM(filter_taps.shape, F32),
            pltpu.VMEM((columns, 8, LANES), F32),
            pltpu.VMEM((seqs, 8, LANES), F32),
            pltpu.VMEM((total_lags, LANES), F32),
            pltpu.VMEM((tiles, group, LANES), F32),
            pltpu.VMEM((group, 2 * SHORT, window), BF16),
            pltpu.VMEM(((2 * ROW + 3) * group, LANES), F32),
            pltpu.VMEM((2 * ROW * group, LANES), F32),
            pltpu.VMEM((group, SHORT, window), BF16),
            pltpu.VMEM((2 * ROW * group, LANES), F32),
            two, two, one,
            pltpu.VMEM((tiles, group * 8, LANES), F32),
            pltpu.VMEM((total_lags, LANES), F32),
            pltpu.VMEM((seqs, 8, LANES), F32),
            pltpu.VMEM((seqs, 8, LANES), F32),
            pltpu.VMEM(filter_taps.shape, F32),
            pltpu.SemaphoreType.DMA((12,)),
            pltpu.SemaphoreType.DMA((12,)),
        ],
        compiler_params=pltpu.CompilerParams(
            collective_id=0, has_side_effects=True, vmem_limit_bytes=48 * 1024 * 1024
        ),
    )(inputs, grad_output, filter_taps)


def solution(mesh):
    return jax.shard_map(
        functools.partial(per_device, seqs=mesh.shape["seq"], chans=mesh.shape["chan"]),
        mesh=mesh,
        in_specs=(P(("seq", "chan"), None), P(("seq", "chan"), None), P("seq", "chan")),
        out_specs=(P(("seq", "chan"), None), P("seq", "chan")),
        check_vma=False,
    )
```

```python
import functools

import jax
import jax.numpy as jnp
from jax import lax
from jax.experimental import pallas as pl
from jax.experimental.pallas import tpu as pltpu
from jax.sharding import PartitionSpec as P

MESH = pl.DeviceIdType.MESH
F32 = jnp.float32
BF16 = jnp.bfloat16
LANES = 128
HALF = LANES // 2
CORES = 2
ROW = 4
PLANES = 4
SHORT = 32
FOLDS = LANES // SHORT

G_ONE, X_ONE, TAPS, G_TWO, X_TWO, HALO_EVEN, HALO_ODD, GI_TWO, GI_ONE, GF, TAPS_IN, GF_OUT = range(12)


def contract(lhs, rhs, lhs_dim, rhs_dim):
    return lax.dot_general(
        lhs, rhs, (((lhs_dim,), (rhs_dim,)), ((), ())), preferred_element_type=F32
    )


def left(values, by):
    return values if by % LANES == 0 else pltpu.roll(values, LANES - by % LANES, 1)


def kernel(
    x_hbm, g_hbm, taps_hbm, gi_out, gf_out,
    g_one, x_one, g_send, x_send, g_two, g_halo, x_two,
    taps, tap_send, tap_recv, tap_rows, tap_tiles, toeplitz,
    g_wide, x_wide, g_cat, gi_wide, gi_send, gi_two, gi_turn,
    gf_partial, gf_rows, gf_send, gf_recv, gf_own,
    send_sem, recv_sem,
):
    seqs = lax.axis_size("seq")
    chans = lax.axis_size("chan")
    seq = lax.axis_index("seq")
    chan = lax.axis_index("chan")
    core = lax.rem(seq, CORES)
    block = lax.div(seq, CORES)
    plane = lax.div(block, ROW)
    place = lax.rem(block, ROW)
    sibling = 1 - core
    slots = ROW * chans
    slot = place * chans + chan
    columns = CORES * ROW
    lags = taps_hbm.shape[0]
    half_lags = lags // 2
    tap_count = tap_tiles.shape[0]
    group = tap_tiles.shape[1]
    rows_of_x = CORES * ROW

    def received(ref, which):
        pltpu.make_async_copy(ref, ref, recv_sem.at[which]).wait()

    def sent(ref, which):
        pltpu.make_async_copy(ref, ref, send_sem.at[which]).wait()

    def remote(src, dst, which, to_seq, to_chan):
        pltpu.make_async_remote_copy(
            src_ref=src, dst_ref=dst, send_sem=send_sem.at[which], recv_sem=recv_sem.at[which],
            device_id={"seq": to_seq, "chan": to_chan}, device_id_type=MESH,
        ).start()

    def local(src, dst, which):
        pltpu.make_async_copy(src, dst, recv_sem.at[which]).start()

    with jax.named_scope("greet"):
        local(taps_hbm, taps, TAPS_IN)
        barrier = pltpu.get_barrier_semaphore()

        def greet_seq(step, carry):
            pl.semaphore_signal(
                barrier, inc=1, device_id={"seq": lax.rem(seq + step, seqs), "chan": chan}, device_id_type=MESH
            )
            return carry

        def greet_plane(step, carry):
            other = lax.rem(chan + step, chans)
            for index in range(ROW):
                pl.semaphore_signal(
                    barrier,
                    inc=1,
                    device_id={"seq": (plane * ROW + index) * CORES + core, "chan": other},
                    device_id_type=MESH,
                )
            return carry

        lax.fori_loop(1, seqs, greet_seq, 0)
        lax.fori_loop(1, chans, greet_plane, 0)

    first_half = lax.broadcasted_iota(jnp.int32, (8, LANES), 1) < HALF

    with jax.named_scope("pack_taps"):
        received(taps, TAPS_IN)
        nothing = jnp.zeros((8 - half_lags, LANES), F32)
        for tile in range(columns // 2):
            lanes = slice(tile * LANES, (tile + 1) * LANES)
            early = jnp.concatenate([taps[0:half_lags, lanes], nothing], axis=0)
            late = jnp.concatenate([taps[half_lags:lags, lanes], nothing], axis=0)
            tap_send[2 * tile] = jnp.where(first_half, early, left(late, HALF))
            tap_send[2 * tile + 1] = jnp.where(first_half, left(early, HALF), late)

    row = lax.broadcasted_iota(jnp.int32, (LANES, LANES), 0)
    lane = lax.broadcasted_iota(jnp.int32, (LANES, LANES), 1)
    eye = (row == lane).astype(F32).astype(BF16)
    flip = (row + lane == LANES - 1).astype(F32).astype(BF16)

    with jax.named_scope("barrier"):
        pl.semaphore_wait(barrier, seqs - 1 + ROW * (chans - 1))

    def columns_of(ref, index):
        start = lax.rem(index, chans) * (ROW * LANES) + lax.div(index, chans) * LANES
        return ref.at[:, pl.ds(pl.multiple_of(start, LANES), LANES)]

    def to_plane(src_of, dst, which):
        def step(shift, carry):
            index = slot + shift
            index = jnp.where(index >= slots, index - slots, index)
            to = (plane * ROW + lax.div(index, chans)) * CORES + core
            remote(src_of(index), dst, which, to, lax.rem(index, chans))
            return carry

        lax.fori_loop(1, slots, step, 0)
        local(src_of(slot), dst, which)

    def to_sibling(src, dst, which):
        remote(src.at[sibling], dst.at[core], which, block * CORES + sibling, chan)
        local(src.at[core], dst.at[core], which)

    def to_seq(src_of, dst, which):
        def step(shift, carry):
            index = seq + shift
            index = jnp.where(index >= seqs, index - seqs, index)
            remote(src_of(index), dst, which, index, chan)
            return carry

        lax.fori_loop(1, seqs, step, 0)
        local(src_of(seq), dst, which)

    with jax.named_scope("send_one"):
        to_plane(functools.partial(columns_of, g_hbm), g_one.at[slot], G_ONE)
        to_seq(lambda index: tap_send.at[lax.rem(index, columns)], tap_recv.at[seq], TAPS)
        to_plane(functools.partial(columns_of, x_hbm), x_one.at[slot], X_ONE)

    def turn(source, index):
        rows = source[chans * index : chans * (index + 1)].reshape(LANES, LANES)
        return contract(eye, rows, 1, 1).astype(BF16)

    def by_core(rows):
        return rows.reshape(CORES, group, LANES)

    with jax.named_scope("turn_g"):
        received(g_one, G_ONE)
        for index in range(ROW):
            g_send[:, :, index * LANES : (index + 1) * LANES] = by_core(turn(g_one, index))

    with jax.named_scope("send_g_two"):
        to_sibling(g_send, g_two, G_TWO)

        def send_halo(width, which):
            for to_core in range(CORES):
                remote(
                    g_send.at[to_core, :, 0:width], g_halo.at[core, :, 0:width], which,
                    ((plane - 1) * ROW + place) * CORES + to_core, chan,
                )

        @pl.when((plane > 0) & (core == 0))
        def _():
            send_halo(2 * LANES, HALO_EVEN)

        @pl.when((plane > 0) & (core == 1))
        def _():
            send_halo(LANES, HALO_ODD)

    with jax.named_scope("turn_x"):
        received(x_one, X_ONE)
        for index in range(ROW):
            turned = contract(turn(x_one, index), flip, 1, 0).astype(BF16)
            x_send[:, :, index * LANES : (index + 1) * LANES] = by_core(turned)
        to_sibling(x_send, x_two, X_TWO)

    with jax.named_scope("unpack_taps"):
        received(tap_recv, TAPS)
        for lag in range(half_lags):
            rows = tap_recv[:, lag, :]
            tap_rows[pl.ds(lag, seqs, stride=lags), :] = rows
            tap_rows[pl.ds(half_lags + lag, seqs, stride=lags), :] = left(rows, HALF)
        for tile in range(tap_count):
            tap_tiles[tile] = tap_rows[tile * LANES : (tile + 1) * LANES, :].T[0:group, :]

    row = lax.broadcasted_iota(jnp.int32, (SHORT, LANES), 0)
    lane = lax.broadcasted_iota(jnp.int32, (SHORT, LANES), 1)
    ahead = lane >= row
    nothing = jnp.zeros((SHORT, LANES), F32)

    def build(channel):
        rolled = []
        for tile in range(tap_count):
            values = jnp.broadcast_to(tap_tiles[tile, pl.ds(channel, 1), :], (SHORT, LANES))
            rolled.append(pltpu.roll(values, 0, 1, stride=1, stride_axis=0))
        for tile in range(tap_count + 1):
            upper = rolled[tile] if tile < tap_count else nothing
            lower = rolled[tile - 1] if tile > 0 else nothing
            values = jnp.where(ahead, upper, lower)
            high = values.astype(BF16)
            low = (values - high.astype(F32)).astype(BF16)
            toeplitz[channel, 0:SHORT, tile * LANES : (tile + 1) * LANES] = high
            toeplitz[channel, SHORT : 2 * SHORT, tile * LANES : (tile + 1) * LANES] = low

    def for_channels(body, unroll):
        def step(first, carry):
            for extra in range(unroll):
                body(first * unroll + extra)
            return carry

        lax.fori_loop(0, group // unroll, step, 0)

    with jax.named_scope("toeplitz"):
        for_channels(build, 16)

    def widen(source, target, index, from_core, at):
        target[at * group : (at + 1) * group, :] = source[
            from_core, :, index * LANES : (index + 1) * LANES
        ].astype(F32)

    with jax.named_scope("widen_g"):
        received(g_two, G_TWO)
        for index in range(ROW):
            for from_core in range(CORES):
                widen(g_two, g_wide, index, from_core, CORES * index + from_core)

        @pl.when(plane < PLANES - 1)
        def _():
            received(g_halo.at[0], HALO_EVEN)
            received(g_halo.at[1, :, 0:LANES], HALO_ODD)
            widen(g_halo, g_wide, 0, 0, rows_of_x)
            widen(g_halo, g_wide, 0, 1, rows_of_x + 1)
            widen(g_halo, g_wide, 1, 0, rows_of_x + 2)

        @pl.when(plane == PLANES - 1)
        def _():
            g_wide[rows_of_x * group : (rows_of_x + 3) * group, :] = jnp.zeros((3 * group, LANES), F32)

    def strided(channel, blocks_ahead=0):
        return pl.ds(channel + blocks_ahead * group, rows_of_x, stride=group)

    lane_of_row = lax.broadcasted_iota(jnp.int32, (rows_of_x, LANES), 1)
    keep = lane - row < LANES - SHORT + 1

    def window_step(channel):
        blocks = [g_wide[strided(channel, tile), :] for tile in range(tap_count + 1)]
        folds = []
        for fold in range(FOLDS):
            shifted = [left(values, SHORT * fold) for values in blocks]
            if fold > 0:
                near_end = lane_of_row < LANES - SHORT * fold
                shifted = [
                    jnp.where(near_end, shifted[tile], shifted[tile + 1]) for tile in range(tap_count)
                ] + [shifted[tap_count]]
            folds.append(jnp.concatenate(shifted, axis=1))
        g_cat[channel] = jnp.concatenate(folds, axis=0).astype(BF16)

    with jax.named_scope("windows"):
        for_channels(window_step, 16)

    def filter_step(channel):
        source = x_wide[strided(channel), :]
        mine = jnp.concatenate(
            [left(source, LANES - SHORT * (fold + 1)) for fold in range(FOLDS)], axis=0
        ).astype(BF16)
        product = contract(mine[:, 0:SHORT], g_cat[channel], 0, 0)
        rolled = [
            pltpu.roll(
                product[:, tile * LANES : (tile + 1) * LANES], LANES - SHORT + 1, 1, stride=1, stride_axis=0
            )
            for tile in range(tap_count + 1)
        ]
        for tile in range(tap_count):
            total = jnp.where(keep, rolled[tile], rolled[tile + 1])
            total = (total[0:8] + total[8:16]) + (total[16:24] + total[24:32])
            gf_partial[tile, pl.ds(pl.multiple_of(channel * 8, 8), 8), :] = total

    def inputs_step(channel):
        result = contract(g_cat[channel], toeplitz[channel], 1, 1)
        result = jnp.concatenate([result, jnp.zeros((SHORT, LANES - 2 * SHORT), F32)], axis=1)
        result = result + left(result, SHORT)
        total = result[0:rows_of_x]
        for fold in range(1, FOLDS):
            part = pltpu.roll(result[fold * rows_of_x : (fold + 1) * rows_of_x], SHORT * fold, 1)
            total = jnp.where(lane_of_row < SHORT * fold, total, part)
        gi_wide[strided(channel), :] = total

    filter_first = plane >= PLANES // 2
    filter_turn = jnp.where(filter_first, 0, 1)

    def two_turns(index, carry):
        @pl.when(index == filter_turn)
        def _():
            received(x_two, X_TWO)
            for place_from in range(ROW):
                for from_core in range(CORES):
                    widen(x_two, x_wide, place_from, from_core, CORES * place_from + from_core)
            for_channels(filter_step, 8)
            for tile in range(tap_count):
                total = gf_partial[tile, pl.ds(0, group, stride=8), :]
                for part in range(1, 8):
                    total = total + gf_partial[tile, pl.ds(part, group, stride=8), :]
                total = jnp.concatenate([total, jnp.zeros((LANES - group, LANES), F32)], axis=0)
                gf_rows[tile * LANES : (tile + 1) * LANES, :] = total.T
            for lag in range(half_lags):
                early = gf_rows[pl.ds(lag, seqs, stride=lags), :]
                late = gf_rows[pl.ds(half_lags + lag, seqs, stride=lags), :]
                gf_send[:, lag, :] = early + left(late, HALF)
            for lag in range(half_lags, 8):
                gf_send[:, lag, :] = jnp.zeros((seqs, LANES), F32)
            to_seq(lambda to: gf_send.at[to], gf_recv.at[seq], GF)

        @pl.when(index != filter_turn)
        def _():
            for_channels(inputs_step, 16)
            for place_to in range(ROW):
                for to_core in range(CORES):
                    start = (CORES * place_to + to_core) * group
                    gi_send[to_core, :, place_to * LANES : (place_to + 1) * LANES] = gi_wide[
                        start : start + group, :
                    ].astype(BF16)
            to_sibling(gi_send, gi_two, GI_TWO)

        return carry

    with jax.named_scope("both_gradients"):
        lax.fori_loop(0, 2, two_turns, 0)

    with jax.named_scope("turn_gi"):
        received(gi_two, GI_TWO)
        for index in range(ROW):
            rows = gi_two[:, :, index * LANES : (index + 1) * LANES].reshape(LANES, LANES)
            turned = contract(eye, rows, 1, 1).astype(BF16)
            gi_turn[chans * index : chans * (index + 1)] = turned.reshape(chans, LANES // chans, LANES)
        to_plane(lambda index: gi_turn.at[index], columns_of(gi_out, slot), GI_ONE)

    with jax.named_scope("unpack_gf"):
        received(gf_recv, GF)
        sums = []
        for index in range(columns):
            total = gf_recv[index]
            for other in range(1, PLANES):
                total = total + gf_recv[other * columns + index]
            sums.append(total)
        for tile in range(columns // 2):
            lanes = slice(tile * LANES, (tile + 1) * LANES)
            early = jnp.where(first_half, sums[2 * tile], left(sums[2 * tile + 1], HALF))
            late = jnp.where(first_half, left(sums[2 * tile], HALF), sums[2 * tile + 1])
            gf_own[0:half_lags, lanes] = early[0:half_lags]
            gf_own[half_lags:lags, lanes] = late[0:half_lags]
        local(gf_own, gf_out, GF_OUT)

    with jax.named_scope("finish"):
        for ref, which in (
            (g_one, G_ONE), (x_one, X_ONE), (tap_recv, TAPS), (g_send, G_TWO), (x_send, X_TWO),
            (gi_send, GI_TWO), (gi_turn, GI_ONE), (gf_send, GF),
        ):
            sent(ref.at[pl.ds(0, ref.shape[0] - 1)], which)

        @pl.when((plane > 0) & (core == 0))
        def _():
            sent(g_send.at[:, :, 0 : 2 * LANES], HALO_EVEN)

        @pl.when((plane > 0) & (core == 1))
        def _():
            sent(g_send.at[:, :, 0:LANES], HALO_ODD)

        received(gf_out, GF_OUT)
        received(gi_out, GI_ONE)


def per_device(inputs, grad_output, filter_taps, seqs, chans):
    rows, channels = inputs.shape
    lags, tap_channels = filter_taps.shape
    slots = ROW * chans
    group = channels // (slots * CORES)
    columns = CORES * ROW
    total_lags = lags * seqs
    tiles = total_lags // LANES
    window = total_lags + LANES
    one = pltpu.VMEM((slots, rows, LANES), BF16)
    two = pltpu.VMEM((CORES, group, ROW * LANES), BF16)
    return pl.pallas_call(
        kernel,
        out_shape=(
            jax.ShapeDtypeStruct(inputs.shape, BF16),
            jax.ShapeDtypeStruct(filter_taps.shape, F32),
        ),
        in_specs=[pl.BlockSpec(memory_space=pl.ANY)] * 3,
        out_specs=(pl.BlockSpec(memory_space=pl.ANY), pl.BlockSpec(memory_space=pl.ANY)),
        scratch_shapes=[
            one, one, two, two, two,
            pltpu.VMEM((CORES, group, 2 * LANES), BF16),
            two,
            pltpu.VMEM(filter_taps.shape, F32),
            pltpu.VMEM((columns, 8, LANES), F32),
            pltpu.VMEM((seqs, 8, LANES), F32),
            pltpu.VMEM((total_lags, LANES), F32),
            pltpu.VMEM((tiles, group, LANES), F32),
            pltpu.VMEM((group, 2 * SHORT, window), BF16),
            pltpu.VMEM(((2 * ROW + 3) * group, LANES), F32),
            pltpu.VMEM((2 * ROW * group, LANES), F32),
            pltpu.VMEM((group, SHORT, window), BF16),
            pltpu.VMEM((2 * ROW * group, LANES), F32),
            two, two, one,
            pltpu.VMEM((tiles, group * 8, LANES), F32),
            pltpu.VMEM((total_lags, LANES), F32),
            pltpu.VMEM((seqs, 8, LANES), F32),
            pltpu.VMEM((seqs, 8, LANES), F32),
            pltpu.VMEM(filter_taps.shape, F32),
            pltpu.SemaphoreType.DMA((12,)),
            pltpu.SemaphoreType.DMA((12,)),
        ],
        compiler_params=pltpu.CompilerParams(
            collective_id=0, has_side_effects=True, vmem_limit_bytes=48 * 1024 * 1024
        ),
    )(*(pltpu.with_memory_space_constraint(array, pltpu.HBM) for array in (inputs, grad_output, filter_taps)))


def solution(mesh):
    return jax.shard_map(
        functools.partial(per_device, seqs=mesh.shape["seq"], chans=mesh.shape["chan"]),
        mesh=mesh,
        in_specs=(P(("seq", "chan"), None), P(("seq", "chan"), None), P("seq", "chan")),
        out_specs=(P(("seq", "chan"), None), P("seq", "chan")),
        check_vma=False,
    )
```

```python
import functools

import jax
import jax.numpy as jnp
from jax import lax
from jax.experimental import pallas as pl
from jax.experimental.pallas import tpu as pltpu
from jax.sharding import PartitionSpec as P

MESH = pl.DeviceIdType.MESH
F32 = jnp.float32
BF16 = jnp.bfloat16
LANES = 128
HALF = LANES // 2
CORES = 2
ROW = 4
PLANES = 4
SHORT = 32
FOLDS = LANES // SHORT

G_ONE, X_ONE, TAPS, G_TWO, X_TWO, HALO_EVEN, HALO_ODD, GI_TWO, GI_ONE, GF, TAPS_IN, GF_OUT, G_IN, X_IN = range(14)


def contract(lhs, rhs, lhs_dim, rhs_dim):
    return lax.dot_general(
        lhs, rhs, (((lhs_dim,), (rhs_dim,)), ((), ())), preferred_element_type=F32
    )


def left(values, by):
    return values if by % LANES == 0 else pltpu.roll(values, LANES - by % LANES, 1)


def kernel(
    x_hbm, g_hbm, taps_hbm, gi_out, gf_out,
    g_own, x_own, g_one, x_one, g_send, x_send, g_two, g_halo, x_two,
    taps, tap_send, tap_recv, tap_rows, tap_tiles, toeplitz,
    g_wide, x_wide, gi_wide, gi_send, gi_two, gi_turn,
    gf_partial, gf_rows, gf_send, gf_recv, gf_own,
    send_sem, recv_sem,
):
    seqs = lax.axis_size("seq")
    chans = lax.axis_size("chan")
    seq = lax.axis_index("seq")
    chan = lax.axis_index("chan")
    core = lax.rem(seq, CORES)
    block = lax.div(seq, CORES)
    plane = lax.div(block, ROW)
    place = lax.rem(block, ROW)
    sibling = 1 - core
    slots = ROW * chans
    slot = place * chans + chan
    columns = CORES * ROW
    lags = taps_hbm.shape[0]
    half_lags = lags // 2
    tap_count = tap_tiles.shape[0]
    group = tap_tiles.shape[1]
    rows_of_x = CORES * ROW
    pitch = group

    def received(ref, which):
        pltpu.make_async_copy(ref, ref, recv_sem.at[which]).wait()

    def sent(ref, which):
        pltpu.make_async_copy(ref, ref, send_sem.at[which]).wait()

    def remote(src, dst, which, to_seq, to_chan):
        pltpu.make_async_remote_copy(
            src_ref=src, dst_ref=dst, send_sem=send_sem.at[which], recv_sem=recv_sem.at[which],
            device_id={"seq": to_seq, "chan": to_chan}, device_id_type=MESH,
        ).start()

    def local(src, dst, which):
        pltpu.make_async_copy(src, dst, recv_sem.at[which]).start()

    with jax.named_scope("greet"):
        local(taps_hbm, taps, TAPS_IN)
        local(g_hbm, g_own, G_IN)
        local(x_hbm, x_own, X_IN)
        barrier = pltpu.get_barrier_semaphore()

        def greet_seq(step, carry):
            pl.semaphore_signal(
                barrier, inc=1, device_id={"seq": lax.rem(seq + step, seqs), "chan": chan}, device_id_type=MESH
            )
            return carry

        def greet_plane(step, carry):
            other = lax.rem(chan + step, chans)
            for index in range(ROW):
                pl.semaphore_signal(
                    barrier,
                    inc=1,
                    device_id={"seq": (plane * ROW + index) * CORES + core, "chan": other},
                    device_id_type=MESH,
                )
            return carry

        lax.fori_loop(1, seqs, greet_seq, 0)
        lax.fori_loop(1, chans, greet_plane, 0)

    first_half = lax.broadcasted_iota(jnp.int32, (8, LANES), 1) < HALF

    with jax.named_scope("pack_taps"):
        received(taps, TAPS_IN)
        nothing = jnp.zeros((8 - half_lags, LANES), F32)
        for tile in range(columns // 2):
            lanes = slice(tile * LANES, (tile + 1) * LANES)
            early = jnp.concatenate([taps[0:half_lags, lanes], nothing], axis=0)
            late = jnp.concatenate([taps[half_lags:lags, lanes], nothing], axis=0)
            tap_send[2 * tile] = jnp.where(first_half, early, left(late, HALF))
            tap_send[2 * tile + 1] = jnp.where(first_half, left(early, HALF), late)

    row = lax.broadcasted_iota(jnp.int32, (LANES, LANES), 0)
    lane = lax.broadcasted_iota(jnp.int32, (LANES, LANES), 1)
    eye = (row == lane).astype(F32).astype(BF16)
    flip = (row + lane == LANES - 1).astype(F32).astype(BF16)

    received(g_own, G_IN)
    received(x_own, X_IN)
    with jax.named_scope("barrier"):
        pl.semaphore_wait(barrier, seqs - 1 + ROW * (chans - 1))

    def columns_of(ref, index):
        start = lax.rem(index, chans) * (ROW * LANES) + lax.div(index, chans) * LANES
        return ref.at[:, pl.ds(pl.multiple_of(start, LANES), LANES)]

    def for_others(count, body):
        def step(first, carry):
            for extra in range(1, 5):
                body(first * 4 + extra)
            return carry

        lax.fori_loop(0, (count - 1) // 4, step, 0)
        for shift in range((count - 1) // 4 * 4 + 1, count):
            body(shift)

    def to_plane(src_of, dst, which):
        def step(shift):
            index = slot + shift
            index = jnp.where(index >= slots, index - slots, index)
            to = (plane * ROW + lax.div(index, chans)) * CORES + core
            remote(src_of(index), dst, which, to, lax.rem(index, chans))

        for_others(slots, step)
        local(src_of(slot), dst, which)

    def to_sibling(src, dst, which):
        remote(src.at[sibling], dst.at[core], which, block * CORES + sibling, chan)
        local(src.at[core], dst.at[core], which)

    def to_seq(src_of, dst, which):
        def step(shift):
            index = seq + shift
            index = jnp.where(index >= seqs, index - seqs, index)
            remote(src_of(index), dst, which, index, chan)

        for_others(seqs, step)
        local(src_of(seq), dst, which)

    with jax.named_scope("send_one"):
        to_plane(functools.partial(columns_of, g_own), g_one.at[slot], G_ONE)
        to_seq(lambda index: tap_send.at[lax.rem(index, columns)], tap_recv.at[seq], TAPS)
        to_plane(functools.partial(columns_of, x_own), x_one.at[slot], X_ONE)

    def turn(source, index):
        rows = source[chans * index : chans * (index + 1)].reshape(LANES, LANES)
        return contract(eye, rows, 1, 1).astype(BF16)

    def by_core(rows):
        return rows.reshape(CORES, group, LANES)

    with jax.named_scope("turn_g"):
        received(g_one, G_ONE)
        for index in range(ROW):
            g_send[:, :, index * LANES : (index + 1) * LANES] = by_core(turn(g_one, index))

    with jax.named_scope("send_g_two"):
        to_sibling(g_send, g_two, G_TWO)

        def send_halo(width, which):
            for to_core in range(CORES):
                remote(
                    g_send.at[to_core, :, 0:width], g_halo.at[core, :, 0:width], which,
                    ((plane - 1) * ROW + place) * CORES + to_core, chan,
                )

        @pl.when((plane > 0) & (core == 0))
        def _():
            send_halo(2 * LANES, HALO_EVEN)

        @pl.when((plane > 0) & (core == 1))
        def _():
            send_halo(LANES, HALO_ODD)

    with jax.named_scope("turn_x"):
        received(x_one, X_ONE)
        for index in range(ROW):
            turned = contract(turn(x_one, index), flip, 1, 0).astype(BF16)
            x_send[:, :, index * LANES : (index + 1) * LANES] = by_core(turned)
        to_sibling(x_send, x_two, X_TWO)

    row = lax.broadcasted_iota(jnp.int32, (SHORT, LANES), 0)
    lane = lax.broadcasted_iota(jnp.int32, (SHORT, LANES), 1)
    ahead = lane >= row
    nothing = jnp.zeros((SHORT, LANES), F32)

    def build(channel):
        rolled = []
        for tile in range(tap_count):
            values = jnp.broadcast_to(tap_tiles[tile, pl.ds(channel, 1), :], (SHORT, LANES))
            rolled.append(pltpu.roll(values, 0, 1, stride=1, stride_axis=0))
        for tile in range(tap_count + 1):
            upper = rolled[tile] if tile < tap_count else nothing
            lower = rolled[tile - 1] if tile > 0 else nothing
            values = jnp.where(ahead, upper, lower)
            high = values.astype(BF16)
            low = (values - high.astype(F32)).astype(BF16)
            toeplitz[channel, 0:SHORT, tile * LANES : (tile + 1) * LANES] = high
            toeplitz[channel, SHORT : 2 * SHORT, tile * LANES : (tile + 1) * LANES] = low

    def for_channels(body, unroll):
        def step(first, carry):
            for extra in range(unroll):
                body(first * unroll + extra)
            return carry

        lax.fori_loop(0, group // unroll, step, 0)

    with jax.named_scope("unpack_taps"):
        received(tap_recv, TAPS)
        for lag in range(half_lags):
            rows = tap_recv[:, lag, :]
            tap_rows[pl.ds(lag, seqs, stride=lags), :] = rows
            tap_rows[pl.ds(half_lags + lag, seqs, stride=lags), :] = left(rows, HALF)
        for tile in range(tap_count):
            tap_tiles[tile] = tap_rows[tile * LANES : (tile + 1) * LANES, :].T[0:group, :]

    with jax.named_scope("toeplitz"):
        for_channels(build, 16)

    def widen(source, target, index, from_core, at):
        target[at * pitch : at * pitch + group, :] = source[
            from_core, :, index * LANES : (index + 1) * LANES
        ].astype(F32)

    with jax.named_scope("widen_g"):
        received(g_two, G_TWO)
        for index in range(ROW):
            for from_core in range(CORES):
                widen(g_two, g_wide, index, from_core, CORES * index + from_core)

        @pl.when(plane < PLANES - 1)
        def _():
            received(g_halo.at[0], HALO_EVEN)
            received(g_halo.at[1, :, 0:LANES], HALO_ODD)
            widen(g_halo, g_wide, 0, 0, rows_of_x)
            widen(g_halo, g_wide, 0, 1, rows_of_x + 1)
            widen(g_halo, g_wide, 1, 0, rows_of_x + 2)

        @pl.when(plane == PLANES - 1)
        def _():
            g_wide[rows_of_x * pitch : (rows_of_x + 3) * pitch, :] = jnp.zeros((3 * pitch, LANES), F32)

    def strided(channel, blocks_ahead=0):
        return pl.ds(channel + blocks_ahead * pitch, rows_of_x, stride=pitch)

    lane_of_row = lax.broadcasted_iota(jnp.int32, (rows_of_x, LANES), 1)
    keep = lane - row < LANES - SHORT + 1

    def gradients_step(channel):
        blocks = [g_wide[strided(channel, tile), :] for tile in range(tap_count + 1)]
        folds = []
        for fold in range(FOLDS):
            shifted = [left(values, SHORT * fold) for values in blocks]
            if fold > 0:
                near_end = lane_of_row < LANES - SHORT * fold
                shifted = [
                    jnp.where(near_end, shifted[tile], shifted[tile + 1]) for tile in range(tap_count)
                ] + [shifted[tap_count]]
            folds.append(jnp.concatenate(shifted, axis=1))
        windows = jnp.concatenate(folds, axis=0).astype(BF16)

        result = contract(windows, toeplitz[channel], 1, 1)
        result = jnp.concatenate([result, jnp.zeros((SHORT, LANES - 2 * SHORT), F32)], axis=1)
        result = result + left(result, SHORT)
        total = result[0:rows_of_x]
        for fold in range(1, FOLDS):
            part = pltpu.roll(result[fold * rows_of_x : (fold + 1) * rows_of_x], SHORT * fold, 1)
            total = jnp.where(lane_of_row < SHORT * fold, total, part)
        gi_wide[strided(channel), :] = total

        source = x_wide[strided(channel), :]
        mine = jnp.concatenate(
            [left(source, LANES - SHORT * (fold + 1)) for fold in range(FOLDS)], axis=0
        ).astype(BF16)
        product = contract(mine[:, 0:SHORT], windows, 0, 0)
        rolled = [
            pltpu.roll(
                product[:, tile * LANES : (tile + 1) * LANES], LANES - SHORT + 1, 1, stride=1, stride_axis=0
            )
            for tile in range(tap_count + 1)
        ]
        for tile in range(tap_count):
            total = jnp.where(keep, rolled[tile], rolled[tile + 1])
            total = (total[0:8] + total[8:16]) + (total[16:24] + total[24:32])
            gf_partial[tile, pl.ds(pl.multiple_of(channel * 8, 8), 8), :] = total

    with jax.named_scope("widen_x"):
        received(x_two, X_TWO)
        for index in range(ROW):
            for from_core in range(CORES):
                widen(x_two, x_wide, index, from_core, CORES * index + from_core)

    with jax.named_scope("gradients"):
        for_channels(gradients_step, 16)

    with jax.named_scope("send_gi_two"):
        for index in range(ROW):
            for to_core in range(CORES):
                start = (CORES * index + to_core) * pitch
                gi_send[to_core, :, index * LANES : (index + 1) * LANES] = gi_wide[start : start + group, :].astype(BF16)
        to_sibling(gi_send, gi_two, GI_TWO)

    with jax.named_scope("send_gf"):
        for tile in range(tap_count):
            total = gf_partial[tile, pl.ds(0, group, stride=8), :]
            for part in range(1, 8):
                total = total + gf_partial[tile, pl.ds(part, group, stride=8), :]
            total = jnp.concatenate([total, jnp.zeros((LANES - group, LANES), F32)], axis=0)
            gf_rows[tile * LANES : (tile + 1) * LANES, :] = total.T
        for lag in range(half_lags):
            early = gf_rows[pl.ds(lag, seqs, stride=lags), :]
            late = gf_rows[pl.ds(half_lags + lag, seqs, stride=lags), :]
            gf_send[:, lag, :] = early + left(late, HALF)
        for lag in range(half_lags, 8):
            gf_send[:, lag, :] = jnp.zeros((seqs, LANES), F32)
        to_seq(lambda index: gf_send.at[index], gf_recv.at[seq], GF)

    with jax.named_scope("turn_gi"):
        received(gi_two, GI_TWO)
        for index in range(ROW):
            rows = gi_two[:, :, index * LANES : (index + 1) * LANES].reshape(LANES, LANES)
            turned = contract(eye, rows, 1, 1).astype(BF16)
            gi_turn[chans * index : chans * (index + 1)] = turned.reshape(chans, LANES // chans, LANES)
        to_plane(lambda index: gi_turn.at[index], columns_of(gi_out, slot), GI_ONE)

    with jax.named_scope("unpack_gf"):
        received(gf_recv, GF)
        sums = []
        for index in range(columns):
            total = gf_recv[index]
            for other in range(1, PLANES):
                total = total + gf_recv[other * columns + index]
            sums.append(total)
        for tile in range(columns // 2):
            lanes = slice(tile * LANES, (tile + 1) * LANES)
            early = jnp.where(first_half, sums[2 * tile], left(sums[2 * tile + 1], HALF))
            late = jnp.where(first_half, left(sums[2 * tile], HALF), sums[2 * tile + 1])
            gf_own[0:half_lags, lanes] = early[0:half_lags]
            gf_own[half_lags:lags, lanes] = late[0:half_lags]
        local(gf_own, gf_out, GF_OUT)

    with jax.named_scope("finish"):
        for ref, which in (
            (g_one, G_ONE), (x_one, X_ONE), (tap_recv, TAPS), (g_send, G_TWO), (x_send, X_TWO),
            (gi_send, GI_TWO), (gi_turn, GI_ONE), (gf_send, GF),
        ):
            sent(ref.at[pl.ds(0, ref.shape[0] - 1)], which)

        @pl.when((plane > 0) & (core == 0))
        def _():
            sent(g_send.at[:, :, 0 : 2 * LANES], HALO_EVEN)

        @pl.when((plane > 0) & (core == 1))
        def _():
            sent(g_send.at[:, :, 0:LANES], HALO_ODD)

        received(gf_out, GF_OUT)
        received(gi_out, GI_ONE)


def per_device(inputs, grad_output, filter_taps, seqs, chans):
    rows, channels = inputs.shape
    lags, tap_channels = filter_taps.shape
    slots = ROW * chans
    group = channels // (slots * CORES)
    columns = CORES * ROW
    total_lags = lags * seqs
    tiles = total_lags // LANES
    window = total_lags + LANES
    one = pltpu.VMEM((slots, rows, LANES), BF16)
    two = pltpu.VMEM((CORES, group, ROW * LANES), BF16)
    return pl.pallas_call(
        kernel,
        out_shape=(
            jax.ShapeDtypeStruct(inputs.shape, BF16),
            jax.ShapeDtypeStruct(filter_taps.shape, F32),
        ),
        in_specs=[pl.BlockSpec(memory_space=pl.ANY)] * 3,
        out_specs=(pl.BlockSpec(memory_space=pl.ANY), pl.BlockSpec(memory_space=pl.ANY)),
        scratch_shapes=[
            pltpu.VMEM(inputs.shape, BF16),
            pltpu.VMEM(inputs.shape, BF16),
            one, one, two, two, two,
            pltpu.VMEM((CORES, group, 2 * LANES), BF16),
            two,
            pltpu.VMEM(filter_taps.shape, F32),
            pltpu.VMEM((columns, 8, LANES), F32),
            pltpu.VMEM((seqs, 8, LANES), F32),
            pltpu.VMEM((total_lags, LANES), F32),
            pltpu.VMEM((tiles, group, LANES), F32),
            pltpu.VMEM((group, 2 * SHORT, window), BF16),
            pltpu.VMEM(((2 * ROW + 3) * group, LANES), F32),
            pltpu.VMEM((2 * ROW * group, LANES), F32),
            pltpu.VMEM((2 * ROW * group, LANES), F32),
            two, two, one,
            pltpu.VMEM((tiles, group * 8, LANES), F32),
            pltpu.VMEM((total_lags, LANES), F32),
            pltpu.VMEM((seqs, 8, LANES), F32),
            pltpu.VMEM((seqs, 8, LANES), F32),
            pltpu.VMEM(filter_taps.shape, F32),
            pltpu.SemaphoreType.DMA((14,)),
            pltpu.SemaphoreType.DMA((14,)),
        ],
        compiler_params=pltpu.CompilerParams(
            collective_id=0, has_side_effects=True, vmem_limit_bytes=48 * 1024 * 1024
        ),
    )(*(pltpu.with_memory_space_constraint(array, pltpu.HBM) for array in (inputs, grad_output, filter_taps)))


def solution(mesh):
    return jax.shard_map(
        functools.partial(per_device, seqs=mesh.shape["seq"], chans=mesh.shape["chan"]),
        mesh=mesh,
        in_specs=(P(("seq", "chan"), None), P(("seq", "chan"), None), P("seq", "chan")),
        out_specs=(P(("seq", "chan"), None), P("seq", "chan")),
        check_vma=False,
    )
```

```python
import functools

import jax
import jax.numpy as jnp
from jax import lax
from jax.experimental import pallas as pl
from jax.experimental.pallas import tpu as pltpu
from jax.sharding import PartitionSpec as P

MESH = pl.DeviceIdType.MESH
F32 = jnp.float32
BF16 = jnp.bfloat16
LANES = 128
HALF = LANES // 2
CORES = 2
ROW = 4
PLANES = 4
SHORT = 32
FOLDS = LANES // SHORT
TOGETHER = 16
LAGS = 1

G_ONE, X_ONE, TAPS, G_TWO, X_TWO, HALO_EVEN, HALO_ODD, GI_TWO, GI_ONE, GF, TAPS_IN, GF_OUT, G_IN, X_IN = range(14)


def contract(lhs, rhs, lhs_dim, rhs_dim):
    return lax.dot_general(
        lhs, rhs, (((lhs_dim,), (rhs_dim,)), ((), ())), preferred_element_type=F32
    )


def left(values, by):
    return values if by % LANES == 0 else pltpu.roll(values, LANES - by % LANES, 1)


def kernel(
    x_hbm, g_hbm, taps_hbm, gi_out, gf_recv,
    g_own, x_own, g_one, x_one, g_send, x_send, g_two, g_halo, x_two,
    taps, tap_send, tap_recv, tap_rows, tap_tiles, toeplitz,
    g_wide, x_wide, gi_wide, gi_send, gi_two, gi_turn,
    gf_partial, gf_rows, gf_send,
    send_sem, recv_sem,
):
    seqs = lax.axis_size("seq")
    chans = lax.axis_size("chan")
    seq = lax.axis_index("seq")
    chan = lax.axis_index("chan")
    core = lax.rem(seq, CORES)
    block = lax.div(seq, CORES)
    plane = lax.div(block, ROW)
    place = lax.rem(block, ROW)
    sibling = 1 - core
    slots = ROW * chans
    slot = place * chans + chan
    columns = CORES * ROW
    lags = taps_hbm.shape[0]
    half_lags = lags // 2
    tap_count = tap_tiles.shape[0]
    group = tap_tiles.shape[1]
    rows_of_x = CORES * ROW
    pitch = group

    def received(ref, which):
        pltpu.make_async_copy(ref, ref, recv_sem.at[which]).wait()

    def sent(ref, which):
        pltpu.make_async_copy(ref, ref, send_sem.at[which]).wait()

    def remote(src, dst, which, to_seq, to_chan):
        pltpu.make_async_remote_copy(
            src_ref=src, dst_ref=dst, send_sem=send_sem.at[which], recv_sem=recv_sem.at[which],
            device_id={"seq": to_seq, "chan": to_chan}, device_id_type=MESH,
        ).start()

    def local(src, dst, which):
        pltpu.make_async_copy(src, dst, recv_sem.at[which]).start()

    with jax.named_scope("greet"):
        local(taps_hbm, taps, TAPS_IN)
        local(g_hbm, g_own, G_IN)
        local(x_hbm, x_own, X_IN)
        barrier = pltpu.get_barrier_semaphore()

        def greet_seq(step, carry):
            pl.semaphore_signal(
                barrier, inc=1, device_id={"seq": lax.rem(seq + step, seqs), "chan": chan}, device_id_type=MESH
            )
            return carry

        def greet_plane(step, carry):
            other = lax.rem(chan + step, chans)
            for index in range(ROW):
                pl.semaphore_signal(
                    barrier,
                    inc=1,
                    device_id={"seq": (plane * ROW + index) * CORES + core, "chan": other},
                    device_id_type=MESH,
                )
            return carry

        lax.fori_loop(8, 25, greet_seq, 0)
        lax.fori_loop(1, chans, greet_plane, 0)
        lax.fori_loop(1, 8, greet_seq, 0)
        lax.fori_loop(25, seqs, greet_seq, 0)

    first_half = lax.broadcasted_iota(jnp.int32, (8, LANES), 1) < HALF

    with jax.named_scope("pack_taps"):
        received(taps, TAPS_IN)
        nothing = jnp.zeros((8 - half_lags, LANES), F32)
        for tile in range(columns // 2):
            lanes = slice(tile * LANES, (tile + 1) * LANES)
            early = jnp.concatenate([taps[0:half_lags, lanes], nothing], axis=0)
            late = jnp.concatenate([taps[half_lags:lags, lanes], nothing], axis=0)
            tap_send[2 * tile] = jnp.where(first_half, early, left(late, HALF))
            tap_send[2 * tile + 1] = jnp.where(first_half, left(early, HALF), late)

    row = lax.broadcasted_iota(jnp.int32, (LANES, LANES), 0)
    lane = lax.broadcasted_iota(jnp.int32, (LANES, LANES), 1)
    eye = (row == lane).astype(F32).astype(BF16)
    flip = (row + lane == LANES - 1).astype(F32).astype(BF16)

    received(g_own, G_IN)
    received(x_own, X_IN)
    with jax.named_scope("barrier"):
        pl.semaphore_wait(barrier, seqs - 1 + ROW * (chans - 1))

    def columns_of(ref, index):
        start = lax.rem(index, chans) * (ROW * LANES) + lax.div(index, chans) * LANES
        return ref.at[:, pl.ds(pl.multiple_of(start, LANES), LANES)]

    def for_others(count, body):
        def step(first, carry):
            for extra in range(1, 5):
                body(first * 4 + extra)
            return carry

        lax.fori_loop(0, (count - 1) // 4, step, 0)
        for shift in range((count - 1) // 4 * 4 + 1, count):
            body(shift)

    def to_plane(src_of, dst, which):
        def step(shift):
            index = slot + shift
            index = jnp.where(index >= slots, index - slots, index)
            to = (plane * ROW + lax.div(index, chans)) * CORES + core
            remote(src_of(index), dst, which, to, lax.rem(index, chans))

        for_others(slots, step)
        local(src_of(slot), dst, which)

    def to_sibling(src, dst, which):
        remote(src.at[sibling], dst.at[core], which, block * CORES + sibling, chan)
        local(src.at[core], dst.at[core], which)

    def to_seq(src_of, dst, which):
        def step(shift):
            index = seq + shift
            index = jnp.where(index >= seqs, index - seqs, index)
            remote(src_of(index), dst, which, index, chan)

        for_others(seqs, step)
        local(src_of(seq), dst, which)

    with jax.named_scope("send_one"):
        to_plane(functools.partial(columns_of, g_own), g_one.at[slot], G_ONE)
        to_seq(lambda index: tap_send.at[lax.rem(index, columns), 0:half_lags], tap_recv.at[seq, 0:half_lags], TAPS)
        to_plane(functools.partial(columns_of, x_own), x_one.at[slot], X_ONE)

    def turn(source, index):
        rows = source[chans * index : chans * (index + 1)].reshape(LANES, LANES)
        return contract(eye, rows, 1, 1).astype(BF16)

    def by_core(rows):
        return rows.reshape(CORES, group, LANES)

    with jax.named_scope("turn_g"):
        received(g_one, G_ONE)
        for index in range(ROW):
            g_send[:, :, index * LANES : (index + 1) * LANES] = by_core(turn(g_one, index))

    with jax.named_scope("send_g_two"):
        to_sibling(g_send, g_two, G_TWO)

        def send_halo(width, which):
            for to_core in range(CORES):
                remote(
                    g_send.at[to_core, :, 0:width], g_halo.at[core, :, 0:width], which,
                    ((plane - 1) * ROW + place) * CORES + to_core, chan,
                )

        @pl.when((plane > 0) & (core == 0))
        def _():
            send_halo(2 * LANES, HALO_EVEN)

        @pl.when((plane > 0) & (core == 1))
        def _():
            send_halo(LANES, HALO_ODD)

    with jax.named_scope("turn_x"):
        received(x_one, X_ONE)
        for index in range(ROW):
            turned = contract(turn(x_one, index), flip, 1, 0).astype(BF16)
            x_send[:, :, index * LANES : (index + 1) * LANES] = by_core(turned)
        to_sibling(x_send, x_two, X_TWO)

    row = lax.broadcasted_iota(jnp.int32, (SHORT, LANES), 0)
    lane = lax.broadcasted_iota(jnp.int32, (SHORT, LANES), 1)
    ahead = lane >= row
    nothing = jnp.zeros((SHORT, LANES), F32)

    def build(channel):
        rolled = []
        for tile in range(tap_count):
            values = jnp.broadcast_to(tap_tiles[tile, pl.ds(channel, 1), :], (SHORT, LANES))
            rolled.append(pltpu.roll(values, 0, 1, stride=1, stride_axis=0))
        for tile in range(tap_count + 1):
            upper = rolled[tile] if tile < tap_count else nothing
            lower = rolled[tile - 1] if tile > 0 else nothing
            values = jnp.where(ahead, upper, lower)
            high = values.astype(BF16)
            low = (values - high.astype(F32)).astype(BF16)
            toeplitz[channel, 0:SHORT, tile * LANES : (tile + 1) * LANES] = high
            toeplitz[channel, SHORT : 2 * SHORT, tile * LANES : (tile + 1) * LANES] = low

    def for_channels(body, unroll):
        def step(first, carry):
            for extra in range(unroll):
                body(first * unroll + extra)
            return carry

        lax.fori_loop(0, group // unroll, step, 0)

    with jax.named_scope("unpack_taps"):
        received(tap_recv.at[:, 0:half_lags], TAPS)
        for lag in range(half_lags):
            rows = tap_recv[:, lag, :]
            tap_rows[pl.ds(lag, seqs, stride=lags), :] = rows
            tap_rows[pl.ds(half_lags + lag, seqs, stride=lags), :] = left(rows, HALF)
        for tile in range(tap_count):
            tap_tiles[tile] = tap_rows[tile * LANES : (tile + 1) * LANES, :].T[0:group, :]

    with jax.named_scope("toeplitz"):
        for_channels(build, 16)

    def widen(source, target, index, from_core, at):
        target[at * pitch : at * pitch + group, :] = source[
            from_core, :, index * LANES : (index + 1) * LANES
        ].astype(F32)

    with jax.named_scope("widen_g"):
        received(g_two, G_TWO)
        for index in range(ROW):
            for from_core in range(CORES):
                widen(g_two, g_wide, index, from_core, CORES * index + from_core)

        @pl.when(plane < PLANES - 1)
        def _():
            received(g_halo.at[0], HALO_EVEN)
            received(g_halo.at[1, :, 0:LANES], HALO_ODD)
            widen(g_halo, g_wide, 0, 0, rows_of_x)
            widen(g_halo, g_wide, 0, 1, rows_of_x + 1)
            widen(g_halo, g_wide, 1, 0, rows_of_x + 2)

        @pl.when(plane == PLANES - 1)
        def _():
            g_wide[rows_of_x * pitch : (rows_of_x + 3) * pitch, :] = jnp.zeros((3 * pitch, LANES), F32)

    def strided(channel, blocks_ahead=0):
        return pl.ds(channel + blocks_ahead * pitch, rows_of_x, stride=pitch)

    lane_of_row = lax.broadcasted_iota(jnp.int32, (rows_of_x, LANES), 1)
    keep = lane - row < LANES - SHORT + 1

    def prepare(channel):
        blocks = [g_wide[strided(channel, tile), :] for tile in range(tap_count + 1)]
        folds = []
        for fold in range(FOLDS):
            shifted = [left(values, SHORT * fold) for values in blocks]
            if fold > 0:
                near_end = lane_of_row < LANES - SHORT * fold
                shifted = [
                    jnp.where(near_end, shifted[tile], shifted[tile + 1]) for tile in range(tap_count)
                ] + [shifted[tap_count]]
            folds.append(jnp.concatenate(shifted, axis=1))
        windows = jnp.concatenate(folds, axis=0).astype(BF16)
        source = x_wide[strided(channel), :]
        mine = jnp.concatenate(
            [left(source, LANES - SHORT * (fold + 1)) for fold in range(FOLDS)], axis=0
        ).astype(BF16)
        return windows, mine[:, 0:SHORT]

    def multiply(channel, windows, mine):
        return contract(windows, toeplitz[channel], 1, 1), contract(mine, windows, 0, 0)

    def finish(channel, result, product):
        result = jnp.concatenate([result, jnp.zeros((SHORT, LANES - 2 * SHORT), F32)], axis=1)
        result = result + left(result, SHORT)
        total = result[0:rows_of_x]
        for fold in range(1, FOLDS):
            part = pltpu.roll(result[fold * rows_of_x : (fold + 1) * rows_of_x], SHORT * fold, 1)
            total = jnp.where(lane_of_row < SHORT * fold, total, part)
        gi_wide[strided(channel), :] = total
        rolled = [
            pltpu.roll(
                product[:, tile * LANES : (tile + 1) * LANES], LANES - SHORT + 1, 1, stride=1, stride_axis=0
            )
            for tile in range(tap_count + 1)
        ]
        for tile in range(tap_count):
            total = jnp.where(keep, rolled[tile], rolled[tile + 1])
            total = (total[0:8] + total[8:16]) + (total[16:24] + total[24:32])
            gf_partial[tile, pl.ds(pl.multiple_of(channel * 8, 8), 8), :] = total

    def gradients_group(first, carry):
        ready, done = {}, {}
        for step in range(TOGETHER + 2 * LAGS):
            if step < TOGETHER:
                ready[step] = prepare(first * TOGETHER + step)
            index = step - LAGS
            if 0 <= index < TOGETHER:
                done[index] = multiply(first * TOGETHER + index, *ready.pop(index))
            index = step - 2 * LAGS
            if 0 <= index < TOGETHER:
                finish(first * TOGETHER + index, *done.pop(index))
        return carry

    with jax.named_scope("widen_x"):
        received(x_two, X_TWO)
        for index in range(ROW):
            for from_core in range(CORES):
                widen(x_two, x_wide, index, from_core, CORES * index + from_core)

    with jax.named_scope("gradients"):
        lax.fori_loop(0, group // TOGETHER, gradients_group, 0)

    with jax.named_scope("send_gi_two"):
        for index in range(ROW):
            for to_core in range(CORES):
                start = (CORES * index + to_core) * pitch
                gi_send[to_core, :, index * LANES : (index + 1) * LANES] = gi_wide[start : start + group, :].astype(BF16)
        to_sibling(gi_send, gi_two, GI_TWO)

    with jax.named_scope("send_gf"):
        for tile in range(tap_count):
            total = gf_partial[tile, pl.ds(0, group, stride=8), :]
            for part in range(1, 8):
                total = total + gf_partial[tile, pl.ds(part, group, stride=8), :]
            total = jnp.concatenate([total, jnp.zeros((LANES - group, LANES), F32)], axis=0)
            gf_rows[tile * LANES : (tile + 1) * LANES, :] = total.T
        for lag in range(half_lags):
            early = gf_rows[pl.ds(lag, seqs, stride=lags), :]
            late = gf_rows[pl.ds(half_lags + lag, seqs, stride=lags), :]
            gf_send[:, lag, :] = early + left(late, HALF)
        for lag in range(half_lags, 8):
            gf_send[:, lag, :] = jnp.zeros((seqs, LANES), F32)
        to_seq(lambda index: gf_send.at[index, 0:half_lags], gf_recv.at[seq, 0:half_lags], GF)

    with jax.named_scope("turn_gi"):
        received(gi_two, GI_TWO)
        for index in range(ROW):
            rows = gi_two[:, :, index * LANES : (index + 1) * LANES].reshape(LANES, LANES)
            turned = contract(eye, rows, 1, 1).astype(BF16)
            gi_turn[chans * index : chans * (index + 1)] = turned.reshape(chans, LANES // chans, LANES)
        to_plane(lambda index: gi_turn.at[index], columns_of(gi_out, slot), GI_ONE)

    with jax.named_scope("finish"):
        for ref, which in (
            (g_one, G_ONE), (x_one, X_ONE), (tap_recv.at[:, 0:half_lags], TAPS), (g_send, G_TWO), (x_send, X_TWO),
            (gi_send, GI_TWO), (gi_turn, GI_ONE), (gf_send.at[:, 0:half_lags], GF),
        ):
            sent(ref.at[pl.ds(0, ref.shape[0] - 1)], which)

        @pl.when((plane > 0) & (core == 0))
        def _():
            sent(g_send.at[:, :, 0 : 2 * LANES], HALO_EVEN)

        @pl.when((plane > 0) & (core == 1))
        def _():
            sent(g_send.at[:, :, 0:LANES], HALO_ODD)

        received(gf_recv.at[:, 0:half_lags], GF)
        received(gi_out, GI_ONE)


def gather_outputs(columns, gi_ref, gf_ref, gi_out, gf_out, gf_own, sem):
    copy = pltpu.make_async_copy(gi_ref, gi_out, sem.at[0])
    copy.start()
    first_half = lax.broadcasted_iota(jnp.int32, (8, LANES), 1) < HALF
    half_lags = gf_own.shape[0] // 2
    sums = []
    for index in range(columns):
        total = gf_ref[index]
        for other in range(1, PLANES):
            total = total + gf_ref[other * columns + index]
        sums.append(total)
    for tile in range(columns // 2):
        lanes = slice(tile * LANES, (tile + 1) * LANES)
        early = jnp.where(first_half, sums[2 * tile], left(sums[2 * tile + 1], HALF))
        late = jnp.where(first_half, left(sums[2 * tile], HALF), sums[2 * tile + 1])
        gf_own[0:half_lags, lanes] = early[0:half_lags]
        gf_own[half_lags : 2 * half_lags, lanes] = late[0:half_lags]
    gf_copy = pltpu.make_async_copy(gf_own, gf_out, sem.at[1])
    gf_copy.start()
    copy.wait()
    gf_copy.wait()


def per_device(inputs, grad_output, filter_taps, seqs, chans):
    rows, channels = inputs.shape
    lags, tap_channels = filter_taps.shape
    slots = ROW * chans
    group = channels // (slots * CORES)
    columns = CORES * ROW
    total_lags = lags * seqs
    tiles = total_lags // LANES
    window = total_lags + LANES
    one = pltpu.VMEM((slots, rows, LANES), BF16)
    two = pltpu.VMEM((CORES, group, ROW * LANES), BF16)
    gi_parts, gf_parts = pl.pallas_call(
        kernel,
        out_shape=(
            jax.ShapeDtypeStruct(inputs.shape, BF16),
            jax.ShapeDtypeStruct((seqs, 8, LANES), F32),
        ),
        in_specs=[pl.BlockSpec(memory_space=pl.ANY)] * 3,
        out_specs=(pl.BlockSpec(memory_space=pl.ANY), pl.BlockSpec(memory_space=pl.ANY)),
        scratch_shapes=[
            pltpu.VMEM(inputs.shape, BF16),
            pltpu.VMEM(inputs.shape, BF16),
            one, one, two, two, two,
            pltpu.VMEM((CORES, group, 2 * LANES), BF16),
            two,
            pltpu.VMEM(filter_taps.shape, F32),
            pltpu.VMEM((columns, 8, LANES), F32),
            pltpu.VMEM((seqs, 8, LANES), F32),
            pltpu.VMEM((total_lags, LANES), F32),
            pltpu.VMEM((tiles, group, LANES), F32),
            pltpu.VMEM((group, 2 * SHORT, window), BF16),
            pltpu.VMEM(((2 * ROW + 3) * group, LANES), F32),
            pltpu.VMEM((2 * ROW * group, LANES), F32),
            pltpu.VMEM((2 * ROW * group, LANES), F32),
            two, two, one,
            pltpu.VMEM((tiles, group * 8, LANES), F32),
            pltpu.VMEM((total_lags, LANES), F32),
            pltpu.VMEM((seqs, 8, LANES), F32),
            pltpu.SemaphoreType.DMA((14,)),
            pltpu.SemaphoreType.DMA((14,)),
        ],
        compiler_params=pltpu.CompilerParams(
            collective_id=0, has_side_effects=True, vmem_limit_bytes=48 * 1024 * 1024
        ),
    )(*(pltpu.with_memory_space_constraint(array, pltpu.HBM) for array in (inputs, grad_output, filter_taps)))
    return pl.pallas_call(
        functools.partial(gather_outputs, columns),
        out_shape=(
            jax.ShapeDtypeStruct(inputs.shape, BF16),
            jax.ShapeDtypeStruct(filter_taps.shape, F32),
        ),
        in_specs=[pl.BlockSpec(memory_space=pltpu.VMEM)] * 2,
        out_specs=(pl.BlockSpec(memory_space=pltpu.HBM), pl.BlockSpec(memory_space=pltpu.HBM)),
        scratch_shapes=[pltpu.VMEM(filter_taps.shape, F32), pltpu.SemaphoreType.DMA((2,))],
        compiler_params=pltpu.CompilerParams(vmem_limit_bytes=16 * 1024 * 1024),
    )(gi_parts, gf_parts)


def solution(mesh):
    return jax.shard_map(
        functools.partial(per_device, seqs=mesh.shape["seq"], chans=mesh.shape["chan"]),
        mesh=mesh,
        in_specs=(P(("seq", "chan"), None), P(("seq", "chan"), None), P("seq", "chan")),
        out_specs=(P(("seq", "chan"), None), P("seq", "chan")),
        check_vma=False,
    )
```

```python
import functools

import jax
import jax.numpy as jnp
from jax import lax
from jax.experimental import pallas as pl
from jax.experimental.pallas import tpu as pltpu
from jax.sharding import PartitionSpec as P

MESH = pl.DeviceIdType.MESH
F32 = jnp.float32
BF16 = jnp.bfloat16
LANES = 128
HALF = LANES // 2
CORES = 2
ROW = 4
PLANES = 4
SHORT = 32
FOLDS = LANES // SHORT
LAGS = 2

G_ONE, X_ONE, TAPS, G_TWO, X_TWO, HALO_EVEN, HALO_ODD, GI_TWO, GI_ONE, GF, TAPS_IN, GF_OUT, G_IN, X_IN = range(14)


def contract(lhs, rhs, lhs_dim, rhs_dim):
    return lax.dot_general(
        lhs, rhs, (((lhs_dim,), (rhs_dim,)), ((), ())), preferred_element_type=F32
    )


def left(values, by):
    return values if by % LANES == 0 else pltpu.roll(values, LANES - by % LANES, 1)


def kernel(
    x_hbm, g_hbm, taps_hbm, gi_out, gf_recv,
    g_own, x_own, g_one, x_one, g_send, x_send, g_two, g_halo, x_two,
    taps, tap_send, tap_recv, tap_rows, tap_tiles, toeplitz,
    g_wide, x_wide, g_cat, x_cat, gi_wide, gi_send, gi_two, gi_turn,
    gf_partial, gf_rows, gf_send,
    send_sem, recv_sem,
):
    seqs = lax.axis_size("seq")
    chans = lax.axis_size("chan")
    seq = lax.axis_index("seq")
    chan = lax.axis_index("chan")
    core = lax.rem(seq, CORES)
    block = lax.div(seq, CORES)
    plane = lax.div(block, ROW)
    place = lax.rem(block, ROW)
    sibling = 1 - core
    slots = ROW * chans
    slot = place * chans + chan
    columns = CORES * ROW
    lags = taps_hbm.shape[0]
    half_lags = lags // 2
    tap_count = tap_tiles.shape[0]
    group = tap_tiles.shape[1]
    rows_of_x = CORES * ROW
    pitch = group

    def received(ref, which):
        pltpu.make_async_copy(ref, ref, recv_sem.at[which]).wait()

    def sent(ref, which):
        pltpu.make_async_copy(ref, ref, send_sem.at[which]).wait()

    def remote(src, dst, which, to_seq, to_chan):
        pltpu.make_async_remote_copy(
            src_ref=src, dst_ref=dst, send_sem=send_sem.at[which], recv_sem=recv_sem.at[which],
            device_id={"seq": to_seq, "chan": to_chan}, device_id_type=MESH,
        ).start()

    def local(src, dst, which):
        pltpu.make_async_copy(src, dst, recv_sem.at[which]).start()

    with jax.named_scope("greet"):
        local(taps_hbm, taps, TAPS_IN)
        local(g_hbm, g_own, G_IN)
        local(x_hbm, x_own, X_IN)
        barrier = pltpu.get_barrier_semaphore()

        def greet_seq(step, carry):
            pl.semaphore_signal(
                barrier, inc=1, device_id={"seq": lax.rem(seq + step, seqs), "chan": chan}, device_id_type=MESH
            )
            return carry

        def greet_plane(step, carry):
            other = lax.rem(chan + step, chans)
            for index in range(ROW):
                pl.semaphore_signal(
                    barrier,
                    inc=1,
                    device_id={"seq": (plane * ROW + index) * CORES + core, "chan": other},
                    device_id_type=MESH,
                )
            return carry

        lax.fori_loop(8, 25, greet_seq, 0)
        lax.fori_loop(1, chans, greet_plane, 0)
        lax.fori_loop(1, 8, greet_seq, 0)
        lax.fori_loop(25, seqs, greet_seq, 0)

    first_half = lax.broadcasted_iota(jnp.int32, (8, LANES), 1) < HALF

    with jax.named_scope("pack_taps"):
        received(taps, TAPS_IN)
        nothing = jnp.zeros((8 - half_lags, LANES), F32)
        for tile in range(columns // 2):
            lanes = slice(tile * LANES, (tile + 1) * LANES)
            early = jnp.concatenate([taps[0:half_lags, lanes], nothing], axis=0)
            late = jnp.concatenate([taps[half_lags:lags, lanes], nothing], axis=0)
            tap_send[2 * tile] = jnp.where(first_half, early, left(late, HALF))
            tap_send[2 * tile + 1] = jnp.where(first_half, left(early, HALF), late)

    row = lax.broadcasted_iota(jnp.int32, (LANES, LANES), 0)
    lane = lax.broadcasted_iota(jnp.int32, (LANES, LANES), 1)
    eye = (row == lane).astype(F32).astype(BF16)
    flip = (row + lane == LANES - 1).astype(F32).astype(BF16)

    received(g_own, G_IN)
    received(x_own, X_IN)
    with jax.named_scope("barrier"):
        pl.semaphore_wait(barrier, seqs - 1 + ROW * (chans - 1))

    def columns_of(ref, index):
        start = lax.rem(index, chans) * (ROW * LANES) + lax.div(index, chans) * LANES
        return ref.at[:, pl.ds(pl.multiple_of(start, LANES), LANES)]

    def for_others(count, body):
        def step(first, carry):
            for extra in range(1, 5):
                body(first * 4 + extra)
            return carry

        lax.fori_loop(0, (count - 1) // 4, step, 0)
        for shift in range((count - 1) // 4 * 4 + 1, count):
            body(shift)

    def to_plane(src_of, dst, which):
        def step(shift):
            index = slot + shift
            index = jnp.where(index >= slots, index - slots, index)
            to = (plane * ROW + lax.div(index, chans)) * CORES + core
            remote(src_of(index), dst, which, to, lax.rem(index, chans))

        for_others(slots, step)
        local(src_of(slot), dst, which)

    def to_sibling(src, dst, which):
        remote(src.at[sibling], dst.at[core], which, block * CORES + sibling, chan)
        local(src.at[core], dst.at[core], which)

    def to_seq(src_of, dst, which):
        def step(shift):
            index = seq + shift
            index = jnp.where(index >= seqs, index - seqs, index)
            remote(src_of(index), dst, which, index, chan)

        for_others(seqs, step)
        local(src_of(seq), dst, which)

    with jax.named_scope("send_one"):
        to_plane(functools.partial(columns_of, g_own), g_one.at[slot], G_ONE)
        to_seq(lambda index: tap_send.at[lax.rem(index, columns), 0:half_lags], tap_recv.at[seq, 0:half_lags], TAPS)
        to_plane(functools.partial(columns_of, x_own), x_one.at[slot], X_ONE)

    def turn(source, index):
        rows = source[chans * index : chans * (index + 1)].reshape(LANES, LANES)
        return contract(eye, rows, 1, 1).astype(BF16)

    def by_core(rows):
        return rows.reshape(CORES, group, LANES)

    with jax.named_scope("turn_g"):
        received(g_one, G_ONE)
        for index in range(ROW):
            g_send[:, :, index * LANES : (index + 1) * LANES] = by_core(turn(g_one, index))

    with jax.named_scope("send_g_two"):
        to_sibling(g_send, g_two, G_TWO)

        def send_halo(width, which):
            for to_core in range(CORES):
                remote(
                    g_send.at[to_core, :, 0:width], g_halo.at[core, :, 0:width], which,
                    ((plane - 1) * ROW + place) * CORES + to_core, chan,
                )

        @pl.when((plane > 0) & (core == 0))
        def _():
            send_halo(2 * LANES, HALO_EVEN)

        @pl.when((plane > 0) & (core == 1))
        def _():
            send_halo(LANES, HALO_ODD)

    with jax.named_scope("turn_x"):
        received(x_one, X_ONE)
        for index in range(ROW):
            turned = contract(turn(x_one, index), flip, 1, 0).astype(BF16)
            x_send[:, :, index * LANES : (index + 1) * LANES] = by_core(turned)
        to_sibling(x_send, x_two, X_TWO)

    row = lax.broadcasted_iota(jnp.int32, (SHORT, LANES), 0)
    lane = lax.broadcasted_iota(jnp.int32, (SHORT, LANES), 1)
    ahead = lane >= row
    nothing = jnp.zeros((SHORT, LANES), F32)

    def build(channel):
        rolled = []
        for tile in range(tap_count):
            values = jnp.broadcast_to(tap_tiles[tile, pl.ds(channel, 1), :], (SHORT, LANES))
            rolled.append(pltpu.roll(values, 0, 1, stride=1, stride_axis=0))
        for tile in range(tap_count + 1):
            upper = rolled[tile] if tile < tap_count else nothing
            lower = rolled[tile - 1] if tile > 0 else nothing
            values = jnp.where(ahead, upper, lower)
            high = values.astype(BF16)
            low = (values - high.astype(F32)).astype(BF16)
            toeplitz[channel, 0:SHORT, tile * LANES : (tile + 1) * LANES] = high
            toeplitz[channel, SHORT : 2 * SHORT, tile * LANES : (tile + 1) * LANES] = low

    def for_channels(body, unroll):
        def step(first, carry):
            for extra in range(unroll):
                body(first * unroll + extra)
            return carry

        lax.fori_loop(0, group // unroll, step, 0)

    with jax.named_scope("unpack_taps"):
        received(tap_recv.at[:, 0:half_lags], TAPS)
        for lag in range(half_lags):
            rows = tap_recv[:, lag, :]
            tap_rows[pl.ds(lag, seqs, stride=lags), :] = rows
            tap_rows[pl.ds(half_lags + lag, seqs, stride=lags), :] = left(rows, HALF)
        for tile in range(tap_count):
            tap_tiles[tile] = tap_rows[tile * LANES : (tile + 1) * LANES, :].T[0:group, :]

    with jax.named_scope("toeplitz"):
        for_channels(build, 64)

    def widen(source, target, index, from_core, at):
        target[at * pitch : at * pitch + group, :] = source[
            from_core, :, index * LANES : (index + 1) * LANES
        ].astype(F32)

    with jax.named_scope("widen_g"):
        received(g_two, G_TWO)
        for index in range(ROW):
            for from_core in range(CORES):
                widen(g_two, g_wide, index, from_core, CORES * index + from_core)

        @pl.when(plane < PLANES - 1)
        def _():
            received(g_halo.at[0], HALO_EVEN)
            received(g_halo.at[1, :, 0:LANES], HALO_ODD)
            widen(g_halo, g_wide, 0, 0, rows_of_x)
            widen(g_halo, g_wide, 0, 1, rows_of_x + 1)
            widen(g_halo, g_wide, 1, 0, rows_of_x + 2)

        @pl.when(plane == PLANES - 1)
        def _():
            g_wide[rows_of_x * pitch : (rows_of_x + 3) * pitch, :] = jnp.zeros((3 * pitch, LANES), F32)

    def strided(channel, blocks_ahead=0):
        return pl.ds(channel + blocks_ahead * pitch, rows_of_x, stride=pitch)

    lane_of_row = lax.broadcasted_iota(jnp.int32, (rows_of_x, LANES), 1)
    keep = lane - row < LANES - SHORT + 1

    def cut_windows(channel):
        blocks = [g_wide[strided(channel, tile), :] for tile in range(tap_count + 1)]
        for fold in range(FOLDS):
            shifted = [left(values, SHORT * fold) for values in blocks]
            if fold > 0:
                near_end = lane_of_row < LANES - SHORT * fold
                shifted = [
                    jnp.where(near_end, shifted[tile], shifted[tile + 1]) for tile in range(tap_count)
                ] + [shifted[tap_count]]
            if fold % 2 == 0:
                before = shifted
                continue
            for tile in range(tap_count + 1):
                g_cat[channel, (fold - 1) * rows_of_x : (fold + 1) * rows_of_x, tile * LANES : (tile + 1) * LANES] = (
                    jnp.concatenate([before[tile], shifted[tile]], axis=0).astype(BF16)
                )

    def cut_x(channel):
        source = x_wide[strided(channel), :]
        x_cat[channel] = jnp.concatenate(
            [left(source, LANES - SHORT * (fold + 1)) for fold in range(FOLDS)], axis=0
        ).astype(BF16)

    def multiply_taps(channel):
        return contract(g_cat[channel], toeplitz[channel], 1, 1)

    def finish_inputs(channel, result):
        result = jnp.concatenate([result, jnp.zeros((SHORT, LANES - 2 * SHORT), F32)], axis=1)
        result = result + left(result, SHORT)
        total = result[0:rows_of_x]
        for fold in range(1, FOLDS):
            part = pltpu.roll(result[fold * rows_of_x : (fold + 1) * rows_of_x], SHORT * fold, 1)
            total = jnp.where(lane_of_row < SHORT * fold, total, part)
        gi_wide[strided(channel), :] = total

    def multiply_x(channel):
        return contract(x_cat[channel, :, 0:SHORT], g_cat[channel], 0, 0)

    def finish_filter(channel, product):
        rolled = [
            pltpu.roll(
                product[:, tile * LANES : (tile + 1) * LANES], LANES - SHORT + 1, 1, stride=1, stride_axis=0
            )
            for tile in range(tap_count + 1)
        ]
        for tile in range(tap_count):
            total = jnp.where(keep, rolled[tile], rolled[tile + 1])
            total = (total[0:8] + total[8:16]) + (total[16:24] + total[24:32])
            gf_partial[tile, pl.ds(pl.multiple_of(channel * 8, 8), 8), :] = total

    def pipelined(multiply, finish, together):
        def step(first, carry):
            done = {}
            for index in range(together + LAGS):
                if index < together:
                    done[index] = multiply(first * together + index)
                if index >= LAGS:
                    finish(first * together + index - LAGS, done.pop(index - LAGS))
            return carry

        lax.fori_loop(0, group // together, step, 0)

    with jax.named_scope("windows"):
        for_channels(cut_windows, 32)

    with jax.named_scope("grad_inputs"):
        pipelined(multiply_taps, finish_inputs, 64)

    with jax.named_scope("send_gi_two"):
        for index in range(ROW):
            for to_core in range(CORES):
                start = (CORES * index + to_core) * pitch
                gi_send[to_core, :, index * LANES : (index + 1) * LANES] = gi_wide[start : start + group, :].astype(BF16)
        to_sibling(gi_send, gi_two, GI_TWO)

    with jax.named_scope("widen_x"):
        received(x_two, X_TWO)
        for index in range(ROW):
            for from_core in range(CORES):
                widen(x_two, x_wide, index, from_core, CORES * index + from_core)

    with jax.named_scope("cut_x"):
        for_channels(cut_x, 32)

    with jax.named_scope("grad_filter"):
        pipelined(multiply_x, finish_filter, 32)

    with jax.named_scope("send_gf"):
        for tile in range(tap_count):
            total = gf_partial[tile, pl.ds(0, group, stride=8), :]
            for part in range(1, 8):
                total = total + gf_partial[tile, pl.ds(part, group, stride=8), :]
            total = jnp.concatenate([total, jnp.zeros((LANES - group, LANES), F32)], axis=0)
            gf_rows[tile * LANES : (tile + 1) * LANES, :] = total.T
        for lag in range(half_lags):
            early = gf_rows[pl.ds(lag, seqs, stride=lags), :]
            late = gf_rows[pl.ds(half_lags + lag, seqs, stride=lags), :]
            gf_send[:, lag, :] = early + left(late, HALF)
        for lag in range(half_lags, 8):
            gf_send[:, lag, :] = jnp.zeros((seqs, LANES), F32)
        to_seq(lambda index: gf_send.at[index, 0:half_lags], gf_recv.at[seq, 0:half_lags], GF)

    with jax.named_scope("turn_gi"):
        received(gi_two, GI_TWO)
        for index in range(ROW):
            rows = gi_two[:, :, index * LANES : (index + 1) * LANES].reshape(LANES, LANES)
            turned = contract(eye, rows, 1, 1).astype(BF16)
            gi_turn[chans * index : chans * (index + 1)] = turned.reshape(chans, LANES // chans, LANES)
        to_plane(lambda index: gi_turn.at[index], columns_of(gi_out, slot), GI_ONE)

    with jax.named_scope("finish"):
        for ref, which in (
            (g_one, G_ONE), (x_one, X_ONE), (tap_recv.at[:, 0:half_lags], TAPS), (g_send, G_TWO), (x_send, X_TWO),
            (gi_send, GI_TWO), (gi_turn, GI_ONE), (gf_send.at[:, 0:half_lags], GF),
        ):
            sent(ref.at[pl.ds(0, ref.shape[0] - 1)], which)

        @pl.when((plane > 0) & (core == 0))
        def _():
            sent(g_send.at[:, :, 0 : 2 * LANES], HALO_EVEN)

        @pl.when((plane > 0) & (core == 1))
        def _():
            sent(g_send.at[:, :, 0:LANES], HALO_ODD)

        received(gf_recv.at[:, 0:half_lags], GF)
        received(gi_out, GI_ONE)


def gather_outputs(columns, gi_ref, gf_ref, gi_out, gf_out, gf_own, sem):
    copy = pltpu.make_async_copy(gi_ref, gi_out, sem.at[0])
    copy.start()
    first_half = lax.broadcasted_iota(jnp.int32, (8, LANES), 1) < HALF
    half_lags = gf_own.shape[0] // 2
    sums = []
    for index in range(columns):
        total = gf_ref[index]
        for other in range(1, PLANES):
            total = total + gf_ref[other * columns + index]
        sums.append(total)
    for tile in range(columns // 2):
        lanes = slice(tile * LANES, (tile + 1) * LANES)
        early = jnp.where(first_half, sums[2 * tile], left(sums[2 * tile + 1], HALF))
        late = jnp.where(first_half, left(sums[2 * tile], HALF), sums[2 * tile + 1])
        gf_own[0:half_lags, lanes] = early[0:half_lags]
        gf_own[half_lags : 2 * half_lags, lanes] = late[0:half_lags]
    gf_copy = pltpu.make_async_copy(gf_own, gf_out, sem.at[1])
    gf_copy.start()
    copy.wait()
    gf_copy.wait()


def per_device(inputs, grad_output, filter_taps, seqs, chans):
    rows, channels = inputs.shape
    lags, tap_channels = filter_taps.shape
    slots = ROW * chans
    group = channels // (slots * CORES)
    columns = CORES * ROW
    total_lags = lags * seqs
    tiles = total_lags // LANES
    window = total_lags + LANES
    one = pltpu.VMEM((slots, rows, LANES), BF16)
    two = pltpu.VMEM((CORES, group, ROW * LANES), BF16)
    gi_parts, gf_parts = pl.pallas_call(
        kernel,
        out_shape=(
            jax.ShapeDtypeStruct(inputs.shape, BF16),
            jax.ShapeDtypeStruct((seqs, 8, LANES), F32),
        ),
        in_specs=[pl.BlockSpec(memory_space=pl.ANY)] * 3,
        out_specs=(pl.BlockSpec(memory_space=pl.ANY), pl.BlockSpec(memory_space=pl.ANY)),
        scratch_shapes=[
            pltpu.VMEM(inputs.shape, BF16),
            pltpu.VMEM(inputs.shape, BF16),
            one, one, two, two, two,
            pltpu.VMEM((CORES, group, 2 * LANES), BF16),
            two,
            pltpu.VMEM(filter_taps.shape, F32),
            pltpu.VMEM((columns, 8, LANES), F32),
            pltpu.VMEM((seqs, 8, LANES), F32),
            pltpu.VMEM((total_lags, LANES), F32),
            pltpu.VMEM((tiles, group, LANES), F32),
            pltpu.VMEM((group, 2 * SHORT, window), BF16),
            pltpu.VMEM(((2 * ROW + 3) * group, LANES), F32),
            pltpu.VMEM((2 * ROW * group, LANES), F32),
            pltpu.VMEM((group, SHORT, window), BF16),
            pltpu.VMEM((group, SHORT, LANES), BF16),
            pltpu.VMEM((2 * ROW * group, LANES), F32),
            two, two, one,
            pltpu.VMEM((tiles, group * 8, LANES), F32),
            pltpu.VMEM((total_lags, LANES), F32),
            pltpu.VMEM((seqs, 8, LANES), F32),
            pltpu.SemaphoreType.DMA((14,)),
            pltpu.SemaphoreType.DMA((14,)),
        ],
        compiler_params=pltpu.CompilerParams(
            collective_id=0, has_side_effects=True, vmem_limit_bytes=48 * 1024 * 1024
        ),
    )(*(pltpu.with_memory_space_constraint(array, pltpu.HBM) for array in (inputs, grad_output, filter_taps)))
    return pl.pallas_call(
        functools.partial(gather_outputs, columns),
        out_shape=(
            jax.ShapeDtypeStruct(inputs.shape, BF16),
            jax.ShapeDtypeStruct(filter_taps.shape, F32),
        ),
        in_specs=[pl.BlockSpec(memory_space=pltpu.VMEM)] * 2,
        out_specs=(pl.BlockSpec(memory_space=pltpu.HBM), pl.BlockSpec(memory_space=pltpu.HBM)),
        scratch_shapes=[pltpu.VMEM(filter_taps.shape, F32), pltpu.SemaphoreType.DMA((2,))],
        compiler_params=pltpu.CompilerParams(vmem_limit_bytes=16 * 1024 * 1024),
    )(gi_parts, gf_parts)


def solution(mesh):
    return jax.shard_map(
        functools.partial(per_device, seqs=mesh.shape["seq"], chans=mesh.shape["chan"]),
        mesh=mesh,
        in_specs=(P(("seq", "chan"), None), P(("seq", "chan"), None), P("seq", "chan")),
        out_specs=(P(("seq", "chan"), None), P("seq", "chan")),
        check_vma=False,
    )
```

```python
import functools

import jax
import jax.numpy as jnp
from jax import lax
from jax.experimental import pallas as pl
from jax.experimental.pallas import tpu as pltpu
from jax.sharding import PartitionSpec as P

MESH = pl.DeviceIdType.MESH
F32 = jnp.float32
BF16 = jnp.bfloat16
LANES = 128
HALF = LANES // 2
CORES = 2
ROW = 4
PLANES = 4
SHORT = 32
FOLDS = LANES // SHORT
LAGS = 2

G_ONE, X_ONE, TAPS, G_TWO, X_TWO, HALO_EVEN, HALO_ODD, GI_TWO, GI_ONE, GF, TAPS_IN, GF_OUT, G_IN, X_IN = range(14)


def contract(lhs, rhs, lhs_dim, rhs_dim):
    return lax.dot_general(
        lhs, rhs, (((lhs_dim,), (rhs_dim,)), ((), ())), preferred_element_type=F32
    )


def left(values, by):
    return values if by % LANES == 0 else pltpu.roll(values, LANES - by % LANES, 1)


def kernel(
    x_hbm, g_hbm, taps_hbm, gi_out, gf_recv,
    g_own, x_own, g_one, x_one, g_send, x_send, g_two, g_halo, x_two,
    taps, tap_send, tap_recv, tap_rows, tap_tiles, toeplitz,
    g_wide, x_wide, g_cat, x_cat, gi_wide, gi_send, gi_two, gi_turn,
    gf_partial, gf_rows, gf_send,
    send_sem, recv_sem,
):
    seqs = lax.axis_size("seq")
    chans = lax.axis_size("chan")
    seq = lax.axis_index("seq")
    chan = lax.axis_index("chan")
    core = lax.rem(seq, CORES)
    block = lax.div(seq, CORES)
    plane = lax.div(block, ROW)
    place = lax.rem(block, ROW)
    sibling = 1 - core
    slots = ROW * chans
    slot = place * chans + chan
    columns = CORES * ROW
    lags = taps_hbm.shape[0]
    half_lags = lags // 2
    tap_count = tap_tiles.shape[0]
    group = tap_tiles.shape[1]
    rows_of_x = CORES * ROW
    pitch = group

    def received(ref, which):
        pltpu.make_async_copy(ref, ref, recv_sem.at[which]).wait()

    def sent(ref, which):
        pltpu.make_async_copy(ref, ref, send_sem.at[which]).wait()

    def remote(src, dst, which, to_seq, to_chan):
        pltpu.make_async_remote_copy(
            src_ref=src, dst_ref=dst, send_sem=send_sem.at[which], recv_sem=recv_sem.at[which],
            device_id={"seq": to_seq, "chan": to_chan}, device_id_type=MESH,
        ).start()

    def local(src, dst, which):
        pltpu.make_async_copy(src, dst, recv_sem.at[which]).start()

    with jax.named_scope("greet"):
        local(taps_hbm, taps, TAPS_IN)
        local(g_hbm, g_own, G_IN)
        local(x_hbm, x_own, X_IN)
        barrier = pltpu.get_barrier_semaphore()

        def greet_seq(step, carry):
            pl.semaphore_signal(
                barrier, inc=1, device_id={"seq": lax.rem(seq + step, seqs), "chan": chan}, device_id_type=MESH
            )
            return carry

        def greet_plane(step, carry):
            other = lax.rem(chan + step, chans)
            for index in range(ROW):
                pl.semaphore_signal(
                    barrier,
                    inc=1,
                    device_id={"seq": (plane * ROW + index) * CORES + core, "chan": other},
                    device_id_type=MESH,
                )
            return carry

        lax.fori_loop(8, 25, greet_seq, 0)
        lax.fori_loop(1, chans, greet_plane, 0)
        lax.fori_loop(1, 8, greet_seq, 0)
        lax.fori_loop(25, seqs, greet_seq, 0)

    first_half = lax.broadcasted_iota(jnp.int32, (8, LANES), 1) < HALF

    with jax.named_scope("pack_taps"):
        received(taps, TAPS_IN)
        nothing = jnp.zeros((8 - half_lags, LANES), F32)
        for tile in range(columns // 2):
            lanes = slice(tile * LANES, (tile + 1) * LANES)
            early = jnp.concatenate([taps[0:half_lags, lanes], nothing], axis=0)
            late = jnp.concatenate([taps[half_lags:lags, lanes], nothing], axis=0)
            tap_send[2 * tile] = jnp.where(first_half, early, left(late, HALF))
            tap_send[2 * tile + 1] = jnp.where(first_half, left(early, HALF), late)

    row = lax.broadcasted_iota(jnp.int32, (LANES, LANES), 0)
    lane = lax.broadcasted_iota(jnp.int32, (LANES, LANES), 1)
    eye = (row == lane).astype(F32).astype(BF16)
    flip = (row + lane == LANES - 1).astype(F32).astype(BF16)

    received(g_own, G_IN)
    received(x_own, X_IN)
    with jax.named_scope("barrier"):
        pl.semaphore_wait(barrier, seqs - 1 + ROW * (chans - 1))

    def columns_of(ref, index):
        start = lax.rem(index, chans) * (ROW * LANES) + lax.div(index, chans) * LANES
        return ref.at[:, pl.ds(pl.multiple_of(start, LANES), LANES)]

    def for_others(count, body):
        for shift in range(1, count):
            body(shift)

    def to_plane(src_of, dst, which):
        def step(shift):
            index = slot + shift
            index = jnp.where(index >= slots, index - slots, index)
            to = (plane * ROW + lax.div(index, chans)) * CORES + core
            remote(src_of(index), dst, which, to, lax.rem(index, chans))

        for_others(slots, step)
        local(src_of(slot), dst, which)

    def to_sibling(src, dst, which):
        remote(src.at[sibling], dst.at[core], which, block * CORES + sibling, chan)
        local(src.at[core], dst.at[core], which)

    def to_seq(src_of, dst, which):
        def step(shift):
            index = seq + shift
            index = jnp.where(index >= seqs, index - seqs, index)
            remote(src_of(index), dst, which, index, chan)

        for_others(seqs, step)
        local(src_of(seq), dst, which)

    with jax.named_scope("send_one"):
        to_plane(functools.partial(columns_of, g_own), g_one.at[slot], G_ONE)
        to_seq(lambda index: tap_send.at[lax.rem(index, columns), 0:half_lags], tap_recv.at[seq, 0:half_lags], TAPS)
        to_plane(functools.partial(columns_of, x_own), x_one.at[slot], X_ONE)

    def turn(source, index):
        rows = source[chans * index : chans * (index + 1)].reshape(LANES, LANES)
        return contract(eye, rows, 1, 1).astype(BF16)

    def by_core(rows):
        return rows.reshape(CORES, group, LANES)

    with jax.named_scope("turn_g"):
        received(g_one, G_ONE)
        for index in range(ROW):
            g_send[:, :, index * LANES : (index + 1) * LANES] = by_core(turn(g_one, index))

    with jax.named_scope("send_g_two"):
        to_sibling(g_send, g_two, G_TWO)

        def send_halo(width, which):
            for to_core in range(CORES):
                remote(
                    g_send.at[to_core, :, 0:width], g_halo.at[core, :, 0:width], which,
                    ((plane - 1) * ROW + place) * CORES + to_core, chan,
                )

        @pl.when((plane > 0) & (core == 0))
        def _():
            send_halo(2 * LANES, HALO_EVEN)

        @pl.when((plane > 0) & (core == 1))
        def _():
            send_halo(LANES, HALO_ODD)

    with jax.named_scope("turn_x"):
        received(x_one, X_ONE)
        for index in range(ROW):
            turned = contract(turn(x_one, index), flip, 1, 0).astype(BF16)
            x_send[:, :, index * LANES : (index + 1) * LANES] = by_core(turned)
        to_sibling(x_send, x_two, X_TWO)

    row = lax.broadcasted_iota(jnp.int32, (SHORT, LANES), 0)
    lane = lax.broadcasted_iota(jnp.int32, (SHORT, LANES), 1)
    ahead = lane >= row
    nothing = jnp.zeros((SHORT, LANES), F32)

    def build(channel):
        rolled = []
        for tile in range(tap_count):
            values = jnp.broadcast_to(tap_tiles[tile, pl.ds(channel, 1), :], (SHORT, LANES))
            rolled.append(pltpu.roll(values, 0, 1, stride=1, stride_axis=0))
        for tile in range(tap_count + 1):
            upper = rolled[tile] if tile < tap_count else nothing
            lower = rolled[tile - 1] if tile > 0 else nothing
            values = jnp.where(ahead, upper, lower)
            high = values.astype(BF16)
            low = (values - high.astype(F32)).astype(BF16)
            toeplitz[channel, 0:SHORT, tile * LANES : (tile + 1) * LANES] = high
            toeplitz[channel, SHORT : 2 * SHORT, tile * LANES : (tile + 1) * LANES] = low

    def for_channels(body, unroll):
        def step(first, carry):
            for extra in range(unroll):
                body(first * unroll + extra)
            return carry

        lax.fori_loop(0, group // unroll, step, 0)

    with jax.named_scope("unpack_taps"):
        received(tap_recv.at[:, 0:half_lags], TAPS)
        for lag in range(half_lags):
            rows = tap_recv[:, lag, :]
            tap_rows[pl.ds(lag, seqs, stride=lags), :] = rows
            tap_rows[pl.ds(half_lags + lag, seqs, stride=lags), :] = left(rows, HALF)
        for tile in range(tap_count):
            tap_tiles[tile] = tap_rows[tile * LANES : (tile + 1) * LANES, :].T[0:group, :]

    with jax.named_scope("toeplitz"):
        for_channels(build, 64)

    def widen(source, target, index, from_core, at):
        target[at * pitch : at * pitch + group, :] = source[
            from_core, :, index * LANES : (index + 1) * LANES
        ].astype(F32)

    with jax.named_scope("widen_g"):
        received(g_two, G_TWO)
        for index in range(ROW):
            for from_core in range(CORES):
                widen(g_two, g_wide, index, from_core, CORES * index + from_core)

        @pl.when(plane < PLANES - 1)
        def _():
            received(g_halo.at[0], HALO_EVEN)
            received(g_halo.at[1, :, 0:LANES], HALO_ODD)
            widen(g_halo, g_wide, 0, 0, rows_of_x)
            widen(g_halo, g_wide, 0, 1, rows_of_x + 1)
            widen(g_halo, g_wide, 1, 0, rows_of_x + 2)

        @pl.when(plane == PLANES - 1)
        def _():
            g_wide[rows_of_x * pitch : (rows_of_x + 3) * pitch, :] = jnp.zeros((3 * pitch, LANES), F32)

    def strided(channel, blocks_ahead=0):
        return pl.ds(channel + blocks_ahead * pitch, rows_of_x, stride=pitch)

    lane_of_row = lax.broadcasted_iota(jnp.int32, (rows_of_x, LANES), 1)
    keep = lane - row < LANES - SHORT + 1

    def cut_windows(channel):
        blocks = [g_wide[strided(channel, tile), :] for tile in range(tap_count + 1)]
        for fold in range(FOLDS):
            shifted = [left(values, SHORT * fold) for values in blocks]
            if fold > 0:
                near_end = lane_of_row < LANES - SHORT * fold
                shifted = [
                    jnp.where(near_end, shifted[tile], shifted[tile + 1]) for tile in range(tap_count)
                ] + [shifted[tap_count]]
            if fold % 2 == 0:
                before = shifted
                continue
            for tile in range(tap_count + 1):
                g_cat[channel, (fold - 1) * rows_of_x : (fold + 1) * rows_of_x, tile * LANES : (tile + 1) * LANES] = (
                    jnp.concatenate([before[tile], shifted[tile]], axis=0).astype(BF16)
                )

    def cut_x(channel):
        source = x_wide[strided(channel), :]
        x_cat[channel] = jnp.concatenate(
            [left(source, LANES - SHORT * (fold + 1)) for fold in range(FOLDS)], axis=0
        ).astype(BF16)

    def multiply_taps(channel):
        windows = g_cat[channel]
        high = contract(windows, toeplitz[channel, 0:SHORT, :], 1, 1)
        return high + contract(windows, toeplitz[channel, SHORT : 2 * SHORT, :], 1, 1)

    def finish_inputs(channel, result):
        result = jnp.concatenate([result, jnp.zeros((SHORT, LANES - SHORT), F32)], axis=1)
        total = result[0:rows_of_x]
        for fold in range(1, FOLDS):
            part = pltpu.roll(result[fold * rows_of_x : (fold + 1) * rows_of_x], SHORT * fold, 1)
            total = jnp.where(lane_of_row < SHORT * fold, total, part)
        gi_wide[strided(channel), :] = total

    def multiply_x(channel):
        return contract(x_cat[channel, :, 0:SHORT], g_cat[channel], 0, 0)

    def finish_filter(channel, product):
        rolled = [
            pltpu.roll(
                product[:, tile * LANES : (tile + 1) * LANES], LANES - SHORT + 1, 1, stride=1, stride_axis=0
            )
            for tile in range(tap_count + 1)
        ]
        for tile in range(tap_count):
            total = jnp.where(keep, rolled[tile], rolled[tile + 1])
            total = (total[0:8] + total[8:16]) + (total[16:24] + total[24:32])
            gf_partial[tile, pl.ds(pl.multiple_of(channel * 8, 8), 8), :] = total

    def pipelined(multiply, finish, together):
        def step(first, carry):
            done = {}
            for index in range(together + LAGS):
                if index < together:
                    done[index] = multiply(first * together + index)
                if index >= LAGS:
                    finish(first * together + index - LAGS, done.pop(index - LAGS))
            return carry

        lax.fori_loop(0, group // together, step, 0)

    with jax.named_scope("windows"):
        for_channels(cut_windows, 32)

    with jax.named_scope("grad_inputs"):
        pipelined(multiply_taps, finish_inputs, 64)

    with jax.named_scope("send_gi_two"):
        for index in range(ROW):
            for to_core in range(CORES):
                start = (CORES * index + to_core) * pitch
                gi_send[to_core, :, index * LANES : (index + 1) * LANES] = gi_wide[start : start + group, :].astype(BF16)
        to_sibling(gi_send, gi_two, GI_TWO)

    with jax.named_scope("widen_x"):
        received(x_two, X_TWO)
        for index in range(ROW):
            for from_core in range(CORES):
                widen(x_two, x_wide, index, from_core, CORES * index + from_core)

    with jax.named_scope("cut_x"):
        for_channels(cut_x, 32)

    with jax.named_scope("grad_filter"):
        pipelined(multiply_x, finish_filter, 64)

    with jax.named_scope("send_gf"):
        for tile in range(tap_count):
            total = gf_partial[tile, pl.ds(0, group, stride=8), :]
            for part in range(1, 8):
                total = total + gf_partial[tile, pl.ds(part, group, stride=8), :]
            total = jnp.concatenate([total, jnp.zeros((LANES - group, LANES), F32)], axis=0)
            gf_rows[tile * LANES : (tile + 1) * LANES, :] = total.T
        for lag in range(half_lags):
            early = gf_rows[pl.ds(lag, seqs, stride=lags), :]
            late = gf_rows[pl.ds(half_lags + lag, seqs, stride=lags), :]
            gf_send[:, lag, :] = early + left(late, HALF)
        for lag in range(half_lags, 8):
            gf_send[:, lag, :] = jnp.zeros((seqs, LANES), F32)
        to_seq(lambda index: gf_send.at[index, 0:half_lags], gf_recv.at[seq, 0:half_lags], GF)

    with jax.named_scope("turn_gi"):
        received(gi_two, GI_TWO)
        for index in range(ROW):
            rows = gi_two[:, :, index * LANES : (index + 1) * LANES].reshape(LANES, LANES)
            turned = contract(eye, rows, 1, 1).astype(BF16)
            gi_turn[chans * index : chans * (index + 1)] = turned.reshape(chans, LANES // chans, LANES)
        to_plane(lambda index: gi_turn.at[index], columns_of(gi_out, slot), GI_ONE)

    with jax.named_scope("finish"):
        for ref, which in (
            (g_one, G_ONE), (x_one, X_ONE), (tap_recv.at[:, 0:half_lags], TAPS), (g_send, G_TWO), (x_send, X_TWO),
            (gi_send, GI_TWO), (gi_turn, GI_ONE), (gf_send.at[:, 0:half_lags], GF),
        ):
            sent(ref.at[pl.ds(0, ref.shape[0] - 1)], which)

        @pl.when((plane > 0) & (core == 0))
        def _():
            sent(g_send.at[:, :, 0 : 2 * LANES], HALO_EVEN)

        @pl.when((plane > 0) & (core == 1))
        def _():
            sent(g_send.at[:, :, 0:LANES], HALO_ODD)

        received(gf_recv.at[:, 0:half_lags], GF)
        received(gi_out, GI_ONE)


def gather_outputs(columns, gi_ref, gf_ref, gi_out, gf_out, gf_own, sem):
    copy = pltpu.make_async_copy(gi_ref, gi_out, sem.at[0])
    copy.start()
    first_half = lax.broadcasted_iota(jnp.int32, (8, LANES), 1) < HALF
    half_lags = gf_own.shape[0] // 2
    sums = []
    for index in range(columns):
        total = gf_ref[index]
        for other in range(1, PLANES):
            total = total + gf_ref[other * columns + index]
        sums.append(total)
    for tile in range(columns // 2):
        lanes = slice(tile * LANES, (tile + 1) * LANES)
        early = jnp.where(first_half, sums[2 * tile], left(sums[2 * tile + 1], HALF))
        late = jnp.where(first_half, left(sums[2 * tile], HALF), sums[2 * tile + 1])
        gf_own[0:half_lags, lanes] = early[0:half_lags]
        gf_own[half_lags : 2 * half_lags, lanes] = late[0:half_lags]
    gf_copy = pltpu.make_async_copy(gf_own, gf_out, sem.at[1])
    gf_copy.start()
    copy.wait()
    gf_copy.wait()


def per_device(inputs, grad_output, filter_taps, seqs, chans):
    rows, channels = inputs.shape
    lags, tap_channels = filter_taps.shape
    slots = ROW * chans
    group = channels // (slots * CORES)
    columns = CORES * ROW
    total_lags = lags * seqs
    tiles = total_lags // LANES
    window = total_lags + LANES
    one = pltpu.VMEM((slots, rows, LANES), BF16)
    two = pltpu.VMEM((CORES, group, ROW * LANES), BF16)
    gi_parts, gf_parts = pl.pallas_call(
        kernel,
        out_shape=(
            jax.ShapeDtypeStruct(inputs.shape, BF16),
            jax.ShapeDtypeStruct((seqs, 8, LANES), F32),
        ),
        in_specs=[pl.BlockSpec(memory_space=pl.ANY)] * 3,
        out_specs=(pl.BlockSpec(memory_space=pl.ANY), pl.BlockSpec(memory_space=pl.ANY)),
        scratch_shapes=[
            pltpu.VMEM(inputs.shape, BF16),
            pltpu.VMEM(inputs.shape, BF16),
            one, one, two, two, two,
            pltpu.VMEM((CORES, group, 2 * LANES), BF16),
            two,
            pltpu.VMEM(filter_taps.shape, F32),
            pltpu.VMEM((columns, 8, LANES), F32),
            pltpu.VMEM((seqs, 8, LANES), F32),
            pltpu.VMEM((total_lags, LANES), F32),
            pltpu.VMEM((tiles, group, LANES), F32),
            pltpu.VMEM((group, 2 * SHORT, window), BF16),
            pltpu.VMEM(((2 * ROW + 3) * group, LANES), F32),
            pltpu.VMEM((2 * ROW * group, LANES), F32),
            pltpu.VMEM((group, SHORT, window), BF16),
            pltpu.VMEM((group, SHORT, LANES), BF16),
            pltpu.VMEM((2 * ROW * group, LANES), F32),
            two, two, one,
            pltpu.VMEM((tiles, group * 8, LANES), F32),
            pltpu.VMEM((total_lags, LANES), F32),
            pltpu.VMEM((seqs, 8, LANES), F32),
            pltpu.SemaphoreType.DMA((14,)),
            pltpu.SemaphoreType.DMA((14,)),
        ],
        compiler_params=pltpu.CompilerParams(
            collective_id=0, has_side_effects=True, vmem_limit_bytes=48 * 1024 * 1024
        ),
    )(*(pltpu.with_memory_space_constraint(array, pltpu.HBM) for array in (inputs, grad_output, filter_taps)))
    return pl.pallas_call(
        functools.partial(gather_outputs, columns),
        out_shape=(
            jax.ShapeDtypeStruct(inputs.shape, BF16),
            jax.ShapeDtypeStruct(filter_taps.shape, F32),
        ),
        in_specs=[pl.BlockSpec(memory_space=pltpu.VMEM)] * 2,
        out_specs=(pl.BlockSpec(memory_space=pltpu.HBM), pl.BlockSpec(memory_space=pltpu.HBM)),
        scratch_shapes=[pltpu.VMEM(filter_taps.shape, F32), pltpu.SemaphoreType.DMA((2,))],
        compiler_params=pltpu.CompilerParams(vmem_limit_bytes=16 * 1024 * 1024),
    )(gi_parts, gf_parts)


def solution(mesh):
    return jax.shard_map(
        functools.partial(per_device, seqs=mesh.shape["seq"], chans=mesh.shape["chan"]),
        mesh=mesh,
        in_specs=(P(("seq", "chan"), None), P(("seq", "chan"), None), P("seq", "chan")),
        out_specs=(P(("seq", "chan"), None), P("seq", "chan")),
        check_vma=False,
    )
```

```python
import functools

import jax
import jax.numpy as jnp
from jax import lax
from jax.experimental import pallas as pl
from jax.experimental.pallas import tpu as pltpu
from jax.sharding import PartitionSpec as P

MESH = pl.DeviceIdType.MESH
F32 = jnp.float32
BF16 = jnp.bfloat16
LANES = 128
HALF = LANES // 2
CORES = 2
ROW = 4
PLANES = 4
SHORT = 32
FOLDS = LANES // SHORT
LAGS = 2

G_ONE, X_ONE, TAPS, G_TWO, X_TWO, HALO_EVEN, HALO_ODD, GI_TWO, GI_ONE, GF, TAPS_IN, GF_OUT, G_IN, X_IN = range(14)


def contract(lhs, rhs, lhs_dim, rhs_dim):
    return lax.dot_general(
        lhs, rhs, (((lhs_dim,), (rhs_dim,)), ((), ())), preferred_element_type=F32
    )


def left(values, by):
    return values if by % LANES == 0 else pltpu.roll(values, LANES - by % LANES, 1)


def kernel(
    x_hbm, g_hbm, taps_hbm, gi_out, gf_recv,
    g_own, x_own, g_one, x_one, g_send, x_send, g_two, g_halo, x_two,
    taps, tap_send, tap_recv, tap_rows, tap_tiles, toeplitz,
    g_wide, x_wide, g_cat, x_cat, gi_wide, gi_send, gi_two, gi_turn,
    gf_partial, gf_rows, gf_send,
    send_sem, recv_sem,
):
    seqs = lax.axis_size("seq")
    chans = lax.axis_size("chan")
    seq = lax.axis_index("seq")
    chan = lax.axis_index("chan")
    core = lax.rem(seq, CORES)
    block = lax.div(seq, CORES)
    plane = lax.div(block, ROW)
    place = lax.rem(block, ROW)
    sibling = 1 - core
    slots = ROW * chans
    slot = place * chans + chan
    columns = CORES * ROW
    lags = taps_hbm.shape[0]
    half_lags = lags // 2
    tap_count = tap_tiles.shape[0]
    group = tap_tiles.shape[1]
    rows_of_x = CORES * ROW
    pitch = group

    def received(ref, which):
        pltpu.make_async_copy(ref, ref, recv_sem.at[which]).wait()

    def sent(ref, which):
        pltpu.make_async_copy(ref, ref, send_sem.at[which]).wait()

    def remote(src, dst, which, to_seq, to_chan):
        pltpu.make_async_remote_copy(
            src_ref=src, dst_ref=dst, send_sem=send_sem.at[which], recv_sem=recv_sem.at[which],
            device_id={"seq": to_seq, "chan": to_chan}, device_id_type=MESH,
        ).start()

    def local(src, dst, which):
        pltpu.make_async_copy(src, dst, recv_sem.at[which]).start()

    with jax.named_scope("greet"):
        local(taps_hbm, taps, TAPS_IN)
        local(g_hbm, g_own, G_IN)
        local(x_hbm, x_own, X_IN)
        barrier = pltpu.get_barrier_semaphore()

        def greet_seq(step, carry):
            pl.semaphore_signal(
                barrier, inc=1, device_id={"seq": lax.rem(seq + step, seqs), "chan": chan}, device_id_type=MESH
            )
            return carry

        def greet_plane(step, carry):
            other = lax.rem(chan + step, chans)
            for index in range(ROW):
                pl.semaphore_signal(
                    barrier,
                    inc=1,
                    device_id={"seq": (plane * ROW + index) * CORES + core, "chan": other},
                    device_id_type=MESH,
                )
            return carry

        lax.fori_loop(8, 25, greet_seq, 0)
        lax.fori_loop(1, chans, greet_plane, 0)
        lax.fori_loop(1, 8, greet_seq, 0)
        lax.fori_loop(25, seqs, greet_seq, 0)

    first_half = lax.broadcasted_iota(jnp.int32, (8, LANES), 1) < HALF

    with jax.named_scope("pack_taps"):
        received(taps, TAPS_IN)
        nothing = jnp.zeros((8 - half_lags, LANES), F32)
        for tile in range(columns // 2):
            lanes = slice(tile * LANES, (tile + 1) * LANES)
            early = jnp.concatenate([taps[0:half_lags, lanes], nothing], axis=0)
            late = jnp.concatenate([taps[half_lags:lags, lanes], nothing], axis=0)
            tap_send[2 * tile] = jnp.where(first_half, early, left(late, HALF))
            tap_send[2 * tile + 1] = jnp.where(first_half, left(early, HALF), late)

    row = lax.broadcasted_iota(jnp.int32, (LANES, LANES), 0)
    lane = lax.broadcasted_iota(jnp.int32, (LANES, LANES), 1)
    eye = (row == lane).astype(F32).astype(BF16)
    flip = (row + lane == LANES - 1).astype(F32).astype(BF16)

    received(g_own, G_IN)
    received(x_own, X_IN)
    with jax.named_scope("barrier"):
        pl.semaphore_wait(barrier, seqs - 1 + ROW * (chans - 1))

    def columns_of(ref, index):
        start = lax.rem(index, chans) * (ROW * LANES) + lax.div(index, chans) * LANES
        return ref.at[:, pl.ds(pl.multiple_of(start, LANES), LANES)]

    def for_others(count, body):
        for shift in range(1, count):
            body(shift)

    def to_plane(src_of, dst, which):
        def step(shift):
            index = slot + shift
            index = jnp.where(index >= slots, index - slots, index)
            to = (plane * ROW + lax.div(index, chans)) * CORES + core
            remote(src_of(index), dst, which, to, lax.rem(index, chans))

        for_others(slots, step)
        local(src_of(slot), dst, which)

    def to_sibling(src, dst, which):
        remote(src.at[sibling], dst.at[core], which, block * CORES + sibling, chan)
        local(src.at[core], dst.at[core], which)

    def to_seq(src_of, dst, which):
        def step(shift):
            index = seq + shift
            index = jnp.where(index >= seqs, index - seqs, index)
            remote(src_of(index), dst, which, index, chan)

        for_others(seqs, step)
        local(src_of(seq), dst, which)

    with jax.named_scope("send_one"):
        to_plane(functools.partial(columns_of, g_own), g_one.at[slot], G_ONE)
        to_seq(lambda index: tap_send.at[lax.rem(index, columns), 0:half_lags], tap_recv.at[seq, 0:half_lags], TAPS)
        to_plane(functools.partial(columns_of, x_own), x_one.at[slot], X_ONE)

    def turn(source, index):
        rows = source[chans * index : chans * (index + 1)].reshape(LANES, LANES)
        return contract(eye, rows, 1, 1).astype(BF16)

    def by_core(rows):
        return rows.reshape(CORES, group, LANES)

    with jax.named_scope("turn_g"):
        received(g_one, G_ONE)
        for index in range(ROW):
            g_send[:, :, index * LANES : (index + 1) * LANES] = by_core(turn(g_one, index))

    with jax.named_scope("send_g_two"):
        to_sibling(g_send, g_two, G_TWO)

        def send_halo(width, which):
            for to_core in range(CORES):
                remote(
                    g_send.at[to_core, :, 0:width], g_halo.at[core, :, 0:width], which,
                    ((plane - 1) * ROW + place) * CORES + to_core, chan,
                )

        @pl.when((plane > 0) & (core == 0))
        def _():
            send_halo(2 * LANES, HALO_EVEN)

        @pl.when((plane > 0) & (core == 1))
        def _():
            send_halo(LANES, HALO_ODD)

    with jax.named_scope("turn_x"):
        received(x_one, X_ONE)
        for index in range(ROW):
            turned = contract(turn(x_one, index), flip, 1, 0).astype(BF16)
            x_send[:, :, index * LANES : (index + 1) * LANES] = by_core(turned)
        to_sibling(x_send, x_two, X_TWO)

    row = lax.broadcasted_iota(jnp.int32, (SHORT, LANES), 0)
    lane = lax.broadcasted_iota(jnp.int32, (SHORT, LANES), 1)
    ahead = lane >= row
    nothing = jnp.zeros((SHORT, LANES), F32)

    def build(channel):
        rolled = []
        for tile in range(tap_count):
            values = jnp.broadcast_to(tap_tiles[tile, pl.ds(channel, 1), :], (SHORT, LANES))
            rolled.append(pltpu.roll(values, 0, 1, stride=1, stride_axis=0))
        for tile in range(tap_count + 1):
            upper = rolled[tile] if tile < tap_count else nothing
            lower = rolled[tile - 1] if tile > 0 else nothing
            values = jnp.where(ahead, upper, lower)
            high = values.astype(BF16)
            low = (values - high.astype(F32)).astype(BF16)
            toeplitz[channel, 0:SHORT, tile * LANES : (tile + 1) * LANES] = high
            toeplitz[channel, SHORT : 2 * SHORT, tile * LANES : (tile + 1) * LANES] = low

    def for_channels(body, unroll):
        def step(first, carry):
            for extra in range(unroll):
                body(first * unroll + extra)
            return carry

        lax.fori_loop(0, group // unroll, step, 0)

    with jax.named_scope("unpack_taps"):
        received(tap_recv.at[:, 0:half_lags], TAPS)
        for lag in range(half_lags):
            rows = tap_recv[:, lag, :]
            tap_rows[pl.ds(lag, seqs, stride=lags), :] = rows
            tap_rows[pl.ds(half_lags + lag, seqs, stride=lags), :] = left(rows, HALF)
        for tile in range(tap_count):
            tap_tiles[tile] = tap_rows[tile * LANES : (tile + 1) * LANES, :].T[0:group, :]

    with jax.named_scope("toeplitz"):
        for_channels(build, 64)

    def widen(source, target, index, from_core, at):
        target[at * pitch : at * pitch + group, :] = source[
            from_core, :, index * LANES : (index + 1) * LANES
        ].astype(F32)

    with jax.named_scope("widen_g"):
        received(g_two, G_TWO)
        for index in range(ROW):
            for from_core in range(CORES):
                widen(g_two, g_wide, index, from_core, CORES * index + from_core)

        @pl.when(plane < PLANES - 1)
        def _():
            received(g_halo.at[0], HALO_EVEN)
            received(g_halo.at[1, :, 0:LANES], HALO_ODD)
            widen(g_halo, g_wide, 0, 0, rows_of_x)
            widen(g_halo, g_wide, 0, 1, rows_of_x + 1)
            widen(g_halo, g_wide, 1, 0, rows_of_x + 2)

        @pl.when(plane == PLANES - 1)
        def _():
            g_wide[rows_of_x * pitch : (rows_of_x + 3) * pitch, :] = jnp.zeros((3 * pitch, LANES), F32)

    def strided(channel, blocks_ahead=0):
        return pl.ds(channel + blocks_ahead * pitch, rows_of_x, stride=pitch)

    lane_of_row = lax.broadcasted_iota(jnp.int32, (rows_of_x, LANES), 1)
    keep = lane - row < LANES - SHORT + 1

    def cut_windows(channel):
        blocks = [g_wide[strided(channel, tile), :] for tile in range(tap_count + 1)]
        for fold in range(FOLDS):
            shifted = [left(values, SHORT * fold) for values in blocks]
            if fold > 0:
                near_end = lane_of_row < LANES - SHORT * fold
                shifted = [
                    jnp.where(near_end, shifted[tile], shifted[tile + 1]) for tile in range(tap_count)
                ] + [shifted[tap_count]]
            if fold % 2 == 0:
                before = shifted
                continue
            for tile in range(tap_count + 1):
                g_cat[channel, (fold - 1) * rows_of_x : (fold + 1) * rows_of_x, tile * LANES : (tile + 1) * LANES] = (
                    jnp.concatenate([before[tile], shifted[tile]], axis=0).astype(BF16)
                )

    def cut_x(channel):
        source = x_wide[strided(channel), :]
        x_cat[channel] = jnp.concatenate(
            [left(source, LANES - SHORT * (fold + 1)) for fold in range(FOLDS)], axis=0
        ).astype(BF16)

    def multiply_taps(channel):
        windows = g_cat[channel]
        high = contract(windows, toeplitz[channel, 0:SHORT, :], 1, 1)
        return high + contract(windows, toeplitz[channel, SHORT : 2 * SHORT, :], 1, 1)

    def finish_inputs(channel, result):
        result = jnp.concatenate([result, jnp.zeros((SHORT, LANES - SHORT), F32)], axis=1)
        total = result[0:rows_of_x]
        for fold in range(1, FOLDS):
            part = pltpu.roll(result[fold * rows_of_x : (fold + 1) * rows_of_x], SHORT * fold, 1)
            total = jnp.where(lane_of_row < SHORT * fold, total, part)
        gi_wide[strided(channel), :] = total

    def multiply_x(channel):
        return contract(x_cat[channel, :, 0:SHORT], g_cat[channel], 0, 0)

    def finish_filter(channel, product):
        rolled = [
            pltpu.roll(
                product[:, tile * LANES : (tile + 1) * LANES], LANES - SHORT + 1, 1, stride=1, stride_axis=0
            )
            for tile in range(tap_count + 1)
        ]
        for tile in range(tap_count):
            total = jnp.where(keep, rolled[tile], rolled[tile + 1])
            total = (total[0:8] + total[8:16]) + (total[16:24] + total[24:32])
            gf_partial[tile, pl.ds(pl.multiple_of(channel * 8, 8), 8), :] = total

    def pipelined(multiply, finish, together):
        def step(first, carry):
            done = {}
            for index in range(together + LAGS):
                if index < together:
                    done[index] = multiply(first * together + index)
                if index >= LAGS:
                    finish(first * together + index - LAGS, done.pop(index - LAGS))
            return carry

        lax.fori_loop(0, group // together, step, 0)

    with jax.named_scope("windows"):
        for_channels(cut_windows, 32)

    with jax.named_scope("grad_inputs"):
        pipelined(multiply_taps, finish_inputs, 64)

    with jax.named_scope("send_gi_two"):
        for index in range(ROW):
            for to_core in range(CORES):
                start = (CORES * index + to_core) * pitch
                gi_send[to_core, :, index * LANES : (index + 1) * LANES] = gi_wide[start : start + group, :].astype(BF16)
        to_sibling(gi_send, gi_two, GI_TWO)

    with jax.named_scope("widen_x"):
        received(x_two, X_TWO)
        for index in range(ROW):
            for from_core in range(CORES):
                widen(x_two, x_wide, index, from_core, CORES * index + from_core)

    with jax.named_scope("cut_x"):
        for_channels(cut_x, 64)

    with jax.named_scope("grad_filter"):
        pipelined(multiply_x, finish_filter, 64)

    with jax.named_scope("send_gf"):
        for tile in range(tap_count):
            total = gf_partial[tile, pl.ds(0, group, stride=8), :]
            for part in range(1, 8):
                total = total + gf_partial[tile, pl.ds(part, group, stride=8), :]
            total = jnp.concatenate([total, jnp.zeros((LANES - group, LANES), F32)], axis=0)
            gf_rows[tile * LANES : (tile + 1) * LANES, :] = total.T
        for lag in range(half_lags):
            early = gf_rows[pl.ds(lag, seqs, stride=lags), :]
            late = gf_rows[pl.ds(half_lags + lag, seqs, stride=lags), :]
            gf_send[:, lag, :] = early + left(late, HALF)
        for lag in range(half_lags, 8):
            gf_send[:, lag, :] = jnp.zeros((seqs, LANES), F32)
        to_seq(lambda index: gf_send.at[index, 0:half_lags], gf_recv.at[seq, 0:half_lags], GF)

    with jax.named_scope("turn_gi"):
        received(gi_two, GI_TWO)
        for index in range(ROW):
            rows = gi_two[:, :, index * LANES : (index + 1) * LANES].reshape(LANES, LANES)
            turned = contract(eye, rows, 1, 1).astype(BF16)
            gi_turn[chans * index : chans * (index + 1)] = turned.reshape(chans, LANES // chans, LANES)
        to_plane(lambda index: gi_turn.at[index], columns_of(gi_out, slot), GI_ONE)

    with jax.named_scope("finish"):
        for ref, which in (
            (g_one, G_ONE), (x_one, X_ONE), (tap_recv.at[:, 0:half_lags], TAPS), (g_send, G_TWO), (x_send, X_TWO),
            (gi_send, GI_TWO), (gi_turn, GI_ONE), (gf_send.at[:, 0:half_lags], GF),
        ):
            sent(ref.at[pl.ds(0, ref.shape[0] - 1)], which)

        @pl.when((plane > 0) & (core == 0))
        def _():
            sent(g_send.at[:, :, 0 : 2 * LANES], HALO_EVEN)

        @pl.when((plane > 0) & (core == 1))
        def _():
            sent(g_send.at[:, :, 0:LANES], HALO_ODD)

        received(gf_recv.at[:, 0:half_lags], GF)
        received(gi_out, GI_ONE)


def gather_outputs(columns, gi_ref, gf_ref, gi_out, gf_out, gf_own, sem):
    copy = pltpu.make_async_copy(gi_ref, gi_out, sem.at[0])
    copy.start()
    first_half = lax.broadcasted_iota(jnp.int32, (8, LANES), 1) < HALF
    half_lags = gf_own.shape[0] // 2
    sums = []
    for index in range(columns):
        total = gf_ref[index]
        for other in range(1, PLANES):
            total = total + gf_ref[other * columns + index]
        sums.append(total)
    for tile in range(columns // 2):
        lanes = slice(tile * LANES, (tile + 1) * LANES)
        early = jnp.where(first_half, sums[2 * tile], left(sums[2 * tile + 1], HALF))
        late = jnp.where(first_half, left(sums[2 * tile], HALF), sums[2 * tile + 1])
        gf_own[0:half_lags, lanes] = early[0:half_lags]
        gf_own[half_lags : 2 * half_lags, lanes] = late[0:half_lags]
    gf_copy = pltpu.make_async_copy(gf_own, gf_out, sem.at[1])
    gf_copy.start()
    copy.wait()
    gf_copy.wait()


def per_device(inputs, grad_output, filter_taps, seqs, chans):
    rows, channels = inputs.shape
    lags, tap_channels = filter_taps.shape
    slots = ROW * chans
    group = channels // (slots * CORES)
    columns = CORES * ROW
    total_lags = lags * seqs
    tiles = total_lags // LANES
    window = total_lags + LANES
    one = pltpu.VMEM((slots, rows, LANES), BF16)
    two = pltpu.VMEM((CORES, group, ROW * LANES), BF16)
    gi_parts, gf_parts = pl.pallas_call(
        kernel,
        out_shape=(
            jax.ShapeDtypeStruct(inputs.shape, BF16),
            jax.ShapeDtypeStruct((seqs, 8, LANES), F32),
        ),
        in_specs=[pl.BlockSpec(memory_space=pl.ANY)] * 3,
        out_specs=(pl.BlockSpec(memory_space=pl.ANY), pl.BlockSpec(memory_space=pl.ANY)),
        scratch_shapes=[
            pltpu.VMEM(inputs.shape, BF16),
            pltpu.VMEM(inputs.shape, BF16),
            one, one, two, two, two,
            pltpu.VMEM((CORES, group, 2 * LANES), BF16),
            two,
            pltpu.VMEM(filter_taps.shape, F32),
            pltpu.VMEM((columns, 8, LANES), F32),
            pltpu.VMEM((seqs, 8, LANES), F32),
            pltpu.VMEM((total_lags + 16, LANES), F32),
            pltpu.VMEM((tiles, group, LANES), F32),
            pltpu.VMEM((group, 2 * SHORT, window), BF16),
            pltpu.VMEM(((2 * ROW + 4) * group, LANES), F32),
            pltpu.VMEM(((2 * ROW + 1) * group, LANES), F32),
            pltpu.VMEM((group, SHORT, window), BF16),
            pltpu.VMEM((group, SHORT, LANES), BF16),
            pltpu.VMEM(((2 * ROW + 1) * group, LANES), F32),
            two, two, one,
            pltpu.VMEM((tiles, group * 8 + 8, LANES), F32),
            pltpu.VMEM((total_lags + 16, LANES), F32),
            pltpu.VMEM((seqs, 8, LANES), F32),
            pltpu.SemaphoreType.DMA((14,)),
            pltpu.SemaphoreType.DMA((14,)),
        ],
        compiler_params=pltpu.CompilerParams(
            collective_id=0, has_side_effects=True, vmem_limit_bytes=48 * 1024 * 1024
        ),
    )(*(pltpu.with_memory_space_constraint(array, pltpu.HBM) for array in (inputs, grad_output, filter_taps)))
    return pl.pallas_call(
        functools.partial(gather_outputs, columns),
        out_shape=(
            jax.ShapeDtypeStruct(inputs.shape, BF16),
            jax.ShapeDtypeStruct(filter_taps.shape, F32),
        ),
        in_specs=[pl.BlockSpec(memory_space=pltpu.VMEM)] * 2,
        out_specs=(pl.BlockSpec(memory_space=pltpu.HBM), pl.BlockSpec(memory_space=pltpu.HBM)),
        scratch_shapes=[pltpu.VMEM(filter_taps.shape, F32), pltpu.SemaphoreType.DMA((2,))],
        compiler_params=pltpu.CompilerParams(vmem_limit_bytes=16 * 1024 * 1024),
    )(gi_parts, gf_parts)


def solution(mesh):
    return jax.shard_map(
        functools.partial(per_device, seqs=mesh.shape["seq"], chans=mesh.shape["chan"]),
        mesh=mesh,
        in_specs=(P(("seq", "chan"), None), P(("seq", "chan"), None), P("seq", "chan")),
        out_specs=(P(("seq", "chan"), None), P("seq", "chan")),
        check_vma=False,
    )
```
